256 devices in a mesh: dp: 64 (over x, y_hi, z), head: 2 (over core), side: 2 (over y_lo).
Axes of the slice: x: 4, y: 4 (y_hi: 2, y_lo: 2; y = y_hi * 2 + y_lo), z: 8, core: 2. Of those that a mesh axis runs over, the one named last changes fastest.
Arguments:
- queries: bfloat16 [2, 192, 8192], P('side', 'dp', 'head'), may hold values from -160 to 160
- new_keys: bfloat16 [2, 192, 512], P('side', 'dp', 'head'), may hold values from -6 to 6
- new_values: bfloat16 [2, 192, 512], P('side', 'dp', 'head'), may hold values from -6 to 6
- key_cache: bfloat16 [2, 192, 2048, 512], P('side', 'dp', None, 'head'), may hold values from -6 to 6
- value_cache: bfloat16 [2, 192, 2048, 512], P('side', 'dp', None, 'head'), may hold values from -6 to 6
- cache_lengths: int32 [2, 192], P('side', 'dp'), may hold values from 1 to 2048, 196608 in all within a row
- residual: bfloat16 [2, 192, 16384], P(None, None, 'dp'), may hold values from -32 to 32
- norm_gain: bfloat16 [16384], P('dp'), may hold values from 0.099609375 to 1.8984375
- out_weight: bfloat16 [8192, 16384], P(('head', 'side'), 'dp'), may hold values from -0.0625 to 0.0625
- gate_weight: bfloat16 [16384, 13312], P('dp', ('head', 'side')), may hold values from -0.046875 to 0.046875
- up_weight: bfloat16 [16384, 13312], P('dp', ('head', 'side')), may hold values from -0.046875 to 0.046875
- down_weight: bfloat16 [13312, 16384], P(('head', 'side'), 'dp'), may hold values from -0.0546875 to 0.0546875
Outputs:
- layer_out: bfloat16 [2, 192, 16384], P('side', 'dp')
The draws below stay inside these ranges and needn't reach their ends.
Inputs may be any that keep to these rules, and one draw needn't show every extreme that they name: `cache_lengths`: A single row holds 1 to 2048 cached positions. Over the 192 rows of one micro-batch (one line of this array) the lengths add up to 196608, and the longest row of each micro-batch holds exactly 2048.
All inputs are finite; a program needn't handle non-finite values. No bound on the sum of `cache_lengths` on one device may be relied on, other than what follows from the above.
Results may differ from the reference program's by a relative error of at most 0.02.
Values may be sent and summed in bfloat16 or wider, within the bound.
A program may use at most 128 MiB of HBM per device.

```python
import math
import jax
import jax.numpy as jnp
import numpy as np
from jax import lax

D = 16384
HS = 128
QH = 64
KVH = 4
FF = 13312
LEN = 2048
MB = 2
ROWS_MB = 192


def fresh_key_base(key):
    base_key = jax.random.fold_in(key, 1)
    return jnp.clip(jax.random.normal(base_key, (MB, ROWS_MB, KVH * HS), jnp.float32), -6.0, 6.0)


def draw_new_keys(key, part):
    return fresh_key_base(key).astype(jnp.bfloat16)


def draw_queries(key, part):
    key = jax.random.fold_in(key, 5)
    shape = (MB, ROWS_MB, QH * HS)
    drawn = 2.0 * jnp.clip(jax.random.normal(key, shape, jnp.float32), -6.0, 6.0)
    return drawn.astype(jnp.bfloat16)


def draw_key_cache(key, part):
    key = jax.random.fold_in(key, 7)
    shape = (MB, ROWS_MB, LEN, KVH * HS)
    keys = jnp.clip(jax.random.normal(key, shape, jnp.float32), -6.0, 6.0)
    return keys.astype(jnp.bfloat16)


def draw_residual(key, part):
    key = jax.random.fold_in(key, 9)
    row_key, column_key, entry_key = jax.random.split(key, 3)
    row_scale = jnp.exp(jax.random.uniform(row_key, (MB, ROWS_MB, 1), jnp.float32, math.log(0.1), 0.0))
    trend = 3.0 ** (jnp.arange(D, dtype=jnp.float32) / D - 0.5)
    column_scale = jnp.exp(jax.random.uniform(column_key, (1, 1, D), jnp.float32, math.log(0.3), math.log(3.0))) * trend
    entries = jnp.clip(jax.random.normal(entry_key, (MB, ROWS_MB, D), jnp.float32), -6.0, 6.0)
    return (entries * row_scale * column_scale).astype(jnp.bfloat16)


def block_scale(key, shape, pieces, smallest, largest):
    loudness, own = 1.0, jax.random.fold_in(key, 6)
    for position, shards_of in pieces:
        draws = jnp.exp(jax.random.uniform(jax.random.fold_in(own, position), (shards_of,), jnp.float32, smallest / len(pieces), largest / len(pieces)))
        loudness = loudness * jnp.repeat(draws, shape[position] // shards_of).reshape([-1 if axis == position else 1 for axis in range(len(shape))])
    return loudness


def profile(count, total, reach, skew):
    loads = [(1 << 20) // math.isqrt(rank ** skew) + 1 for rank in range(2, count + 1)]
    surplus, given = total - reach - (count - 1), [1] * (count - 1)
    while surplus > 0:
        candidates = [i for i in range(count - 1) if given[i] < reach]
        whole, left = sum([loads[i] for i in candidates]), surplus
        for i in candidates:
            extra = min(reach - given[i], max(1, left * loads[i] // whole), surplus)
            given[i] = given[i] + extra
            surplus = surplus - extra
    return np.array([reach] + given)


def ragged(own_key, number_of, total, reach, slope):
    if number_of == 2:
        one = jax.random.randint(own_key, (), max(1, total - reach), min(reach, total - 1) + 1)
        return jnp.stack([one, total - one])
    lengths = jnp.asarray(profile(number_of, total, reach, slope), jnp.int32)
    pairs = (number_of - 1) // 2
    giver, receiver = lengths[1:1 + 2 * pairs:2], lengths[2:2 + 2 * pairs:2]
    slack = jnp.minimum(giver - 1, reach - receiver)
    shifted = jax.random.randint(jax.random.fold_in(own_key, 1), (pairs,), 0, 1 << 20) % (slack + 1)
    lengths = lengths.at[1:1 + 2 * pairs:2].set(giver - shifted).at[2:2 + 2 * pairs:2].set(receiver + shifted)
    return lengths[jax.random.permutation(jax.random.fold_in(own_key, 2), number_of)]


def bell_draw(stream_key, shape, scale, most, shards=(), held_as=jnp.bfloat16):
    drawn = jax.random.normal(stream_key, shape, jnp.float32) * scale
    if len(shards) > 0:
        drawn = block_scale(stream_key, shape, shards, -0.22, 0.18) * drawn
    return jnp.clip(drawn, min=-most, max=most).astype(held_as)


def setup_inputs(seed: int = 0) -> dict:
    seeds = jax.random.split(jax.random.key(seed), 13)
    queries = draw_queries(jax.random.fold_in(seeds[12], 71), 0)
    new_keys = draw_new_keys(jax.random.fold_in(seeds[12], 71), 0)
    new_values = bell_draw(seeds[2], (MB, ROWS_MB, KVH * HS), 1.0, 6.0, ((0, 2), (1, 64), (2, 2)))
    key_cache = draw_key_cache(jax.random.fold_in(seeds[12], 71), 0)
    value_cache = bell_draw(seeds[4], (MB, ROWS_MB, LEN, KVH * HS), 1.0, 6.0, ((0, 2), (1, 64), (3, 2)))
    cache_lengths = jax.vmap(lambda own: ragged(own, ROWS_MB, ROWS_MB * LEN // 2, LEN, 2))(jax.random.split(seeds[5], MB)).reshape((MB, ROWS_MB)).astype(jnp.int32)
    residual = draw_residual(jax.random.fold_in(seeds[12], 71), 0)
    norm_gain = jnp.clip(1.0 + 0.18 * jax.random.normal(seeds[7], (D,), jnp.float32), 0.099609375, 1.8984375).astype(jnp.bfloat16)
    out_weight = bell_draw(seeds[8], (QH * HS, D), (QH * HS) ** -0.5, 0.0625, ((0, 4), (1, 64)))
    gate_weight = bell_draw(seeds[9], (D, FF), D ** -0.5, 0.046875, ((0, 64), (1, 4)))
    up_weight = bell_draw(seeds[10], (D, FF), D ** -0.5, 0.046875, ((0, 64), (1, 4)))
    down_weight = bell_draw(seeds[11], (FF, D), FF ** -0.5, 0.0546875, ((0, 4), (1, 64)))
    return dict(queries=queries, new_keys=new_keys, new_values=new_values, key_cache=key_cache, value_cache=value_cache, cache_lengths=cache_lengths, residual=residual, norm_gain=norm_gain, out_weight=out_weight, gate_weight=gate_weight, up_weight=up_weight, down_weight=down_weight)


def attend_row(packed):
    query_row, key_row, value_row, key_block, value_block, length = packed
    group = QH // KVH
    query_heads = query_row.astype(jnp.float32).reshape(KVH, group, HS)
    fresh_key = key_row.astype(jnp.float32).reshape(KVH, HS)
    fresh_value = value_row.astype(jnp.float32).reshape(KVH, HS)
    cache_keys = key_block.astype(jnp.float32).reshape(LEN, KVH, HS)
    cache_values = value_block.astype(jnp.float32).reshape(LEN, KVH, HS)
    scale_factor = 1.0 / math.sqrt(HS)
    scores = jnp.einsum('jgd,tjd->jgt', query_heads, cache_keys) * scale_factor
    fresh = jnp.einsum('jgd,jd->jg', query_heads, fresh_key) * scale_factor
    valid = jnp.arange(LEN, dtype=jnp.int32) < length
    masked = jnp.where(valid, scores, -jnp.inf)
    highest = jnp.maximum(lax.optimization_barrier(jnp.max(masked, axis=-1)), fresh)
    probs = jnp.exp(masked - highest[..., None])
    fresh_prob = jnp.exp(fresh - highest)
    total = lax.optimization_barrier(jnp.sum(probs, axis=-1)) + fresh_prob
    weights = (probs / total[..., None]).astype(jnp.bfloat16)
    fresh_weight = (fresh_prob / total).astype(jnp.bfloat16)
    mixed = jnp.einsum('jgt,tjd->jgd', weights.astype(jnp.float32), cache_values)
    mixed = mixed + fresh_weight.astype(jnp.float32)[..., None] * fresh_value[:, None, :]
    return mixed.reshape(QH * HS).astype(jnp.bfloat16)

def reference(queries, new_keys, new_values, key_cache, value_cache, cache_lengths, residual, norm_gain, out_weight, gate_weight, up_weight, down_weight):
    row_total = MB * ROWS_MB
    packed = (queries.reshape(row_total, QH * HS), new_keys.reshape(row_total, KVH * HS), new_values.reshape(row_total, KVH * HS), key_cache.reshape(row_total, LEN, KVH * HS), value_cache.reshape(row_total, LEN, KVH * HS), cache_lengths.reshape(row_total))
    attended = lax.map(attend_row, packed)
    projected = jnp.dot(attended, out_weight, preferred_element_type=jnp.float32)
    hidden_in = residual.astype(jnp.float32).reshape(row_total, D) + projected
    mean_square = lax.optimization_barrier(jnp.mean(hidden_in * hidden_in, axis=-1))
    normed = (hidden_in * lax.rsqrt(mean_square + 1e-05)[:, None] * norm_gain.astype(jnp.float32)).astype(jnp.bfloat16)
    gate = jnp.dot(normed, gate_weight, preferred_element_type=jnp.float32)
    upper = jnp.dot(normed, up_weight, preferred_element_type=jnp.float32)
    act = (jax.nn.silu(gate) * upper).astype(jnp.bfloat16)
    result = hidden_in + jnp.dot(act, down_weight, preferred_element_type=jnp.float32)
    return result.reshape(MB, ROWS_MB, D).astype(jnp.bfloat16)
```

```python
import math

import jax
import jax.numpy as jnp
from jax import lax
from jax.experimental import pallas as pl
from jax.experimental.pallas import tpu as pltpu
from jax.sharding import PartitionSpec as P

D = 16384
HS = 128
BF = jnp.bfloat16
F32 = jnp.float32
MESH = pl.DeviceIdType.MESH
VMEM_LIMIT = 56 * 2**20

NA = 7
NB = 6


def attend_kernel(len_ref, q_ref, nk_ref, nv_ref, k_ref, v_ref, o_ref):
    row = pl.program_id(0)
    length = len_ref[0, row]
    span = k_ref.shape[1]
    q = q_ref[0].astype(F32)
    zero = jnp.zeros_like(q[:16])
    wide = jnp.concatenate(
        [jnp.concatenate([q[:16], zero], axis=1), jnp.concatenate([zero, q[16:]], axis=1)], axis=0
    )
    scale = 1.0 / math.sqrt(HS)
    nt = (((1,), (1,)), ((), ()))
    scores = lax.dot_general(wide.astype(BF), k_ref[0], nt, preferred_element_type=F32) * scale
    fresh = jnp.sum(wide * nk_ref[0].astype(F32), axis=1, keepdims=True) * scale
    valid = lax.broadcasted_iota(jnp.int32, (32, span), 1) < length
    masked = jnp.where(valid, scores, -jnp.inf)
    highest = jnp.maximum(jnp.max(masked, axis=1, keepdims=True), fresh)
    probs = jnp.exp(masked - highest)
    fresh_prob = jnp.exp(fresh - highest)
    total = jnp.sum(probs, axis=1, keepdims=True) + fresh_prob
    inverse = 1.0 / total
    weights = (probs * inverse).astype(BF)
    fresh_weight = (fresh_prob * inverse).astype(BF).astype(F32)
    mixed = jnp.dot(weights, v_ref[0], preferred_element_type=F32)
    mixed = mixed + fresh_weight * nv_ref[0].astype(F32)
    o_ref[0, 0] = mixed[:16, :HS].astype(BF)
    o_ref[0, 1] = mixed[16:, HS:].astype(BF)


def attend(queries, new_keys, new_values, key_cache, value_cache, cache_lengths):
    rows, span = key_cache.shape[1], key_cache.shape[2]
    return pl.pallas_call(
        attend_kernel,
        grid=(rows,),
        in_specs=[
            pl.BlockSpec(memory_space=pltpu.SMEM),
            pl.BlockSpec((1, 32, HS), lambda r: (r, 0, 0)),
            pl.BlockSpec((1, 1, 2 * HS), lambda r: (r, 0, 0)),
            pl.BlockSpec((1, 1, 2 * HS), lambda r: (r, 0, 0)),
            pl.BlockSpec((1, span, 2 * HS), lambda r: (r, 0, 0)),
            pl.BlockSpec((1, span, 2 * HS), lambda r: (r, 0, 0)),
        ],
        out_specs=pl.BlockSpec((1, 2, 16, HS), lambda r: (r, 0, 0, 0)),
        out_shape=jax.ShapeDtypeStruct((rows, 2, 16, HS), BF),
        compiler_params=pltpu.CompilerParams(vmem_limit_bytes=VMEM_LIMIT),
        cost_estimate=pl.CostEstimate(flops=2 * 2 * rows * 32 * span * 256, bytes_accessed=rows * span * 1024, transcendentals=rows * 32 * span),
        name="attend",
    )(
        cache_lengths,
        queries.reshape(rows, 32, HS),
        new_keys.reshape(rows, 1, 2 * HS),
        new_values.reshape(rows, 1, 2 * HS),
        key_cache[0],
        value_cache[0],
    )


def slab_kernel(
    att, res, gain, wo_hbm, wg_hbm, wu_hbm, wd_hbm,
    out,
    wo, wg, wu, wd,
    seen, wide, part, part_bf, quarter_in, hidden, scaled,
    squares, squares_in, squares_all,
    pa, pa_in1, pa_in2, ya, ya_in, za, za_in,
    pb, pb_in, xb, xb_in,
    act_a, act_b, down, down_bf, down_in, fin, send1, mid,
    wsem, ss, rs,
):
    dp = lax.axis_index("dp")
    h = lax.axis_index("head")
    s = lax.axis_index("side")
    z = lax.rem(dp, 8)
    xy = dp // 8
    yh = lax.rem(xy, 2)
    x = xy // 2
    mine = 2 * s + h

    def dev(dx=0, dy=0, dz=0, dh=0, ds=0):
        nx = lax.rem(x + (dx + 4), 4)
        ny = lax.rem(yh + dy, 2)
        nz = lax.rem(z + (dz + 8), 8)
        return ((nx * 2 + ny) * 8 + nz, lax.rem(h + dh, 2), lax.rem(s + ds, 2))

    counter = [0]
    pending = []

    def ids(count):
        first = counter[0]
        counter[0] += count
        return first

    def send(src, dst, target, index, keep=True):
        copy = pltpu.make_async_remote_copy(
            src_ref=src, dst_ref=dst, send_sem=ss.at[index], recv_sem=rs.at[index],
            device_id=target, device_id_type=MESH,
        )
        copy.start()
        if keep:
            pending.append(copy)
        return copy

    def arrived(ref, index):
        pltpu.make_async_remote_copy(
            src_ref=ref, dst_ref=ref, send_sem=ss.at[index], recv_sem=rs.at[index],
            device_id=dev(dh=1), device_id_type=MESH,
        ).wait_recv()

    def left(ref, index):
        pltpu.make_async_remote_copy(
            src_ref=ref, dst_ref=ref, send_sem=ss.at[index], recv_sem=rs.at[index],
            device_id=dev(dh=1), device_id_type=MESH,
        ).wait_send()

    loads = []
    for k, (src, dst) in enumerate(((wo_hbm, wo), (wg_hbm, wg), (wu_hbm, wu), (wd_hbm, wd))):
        copy = pltpu.make_async_copy(src, dst, wsem.at[k])
        copy.start()
        loads.append(copy)

    plane = [(dx, dy) for dx in range(4) for dy in range(2)]
    peers = [dict(dx=dx, dy=dy, dh=dh) for dx, dy in plane for dh in range(2) if dx or dy or dh]
    peers += [dict(dz=dz) for dz in range(1, 8)]
    peers += [dict(ds=1), dict(dh=1, ds=1)]
    barrier = pltpu.get_barrier_semaphore()
    for peer in peers:
        pl.semaphore_signal(barrier, inc=1, device_id=dev(**peer), device_id_type=MESH)
    pl.semaphore_wait(barrier, len(peers))

    side_id = ids(1)
    send(att.at[:, 1 - s], seen.at[s, dp], dev(ds=1), side_id)
    seen[s, dp] = att[:, s]

    y_id = ids(1)
    za_id = ids(8)
    xa_id = ids(8 * 3)
    xyb_id = ids(8)
    zb_id = ids(16)

    def block_a():
        send(seen.at[0, dp], seen.at[0, dp], dev(dy=1), y_id)

    def block_b():
        for k, (dx, dy) in enumerate(plane[1:]):
            send(seen.at[1, dp], seen.at[1, dp], dev(dx=dx, dy=dy), xyb_id + k)

    def slot(nx, ny, nz):
        return (nx * 2 + ny) * 8 + nz

    xs = [lax.rem(x + d, 4) for d in range(4)]
    zs = [lax.rem(z + d, 8) for d in range(8)]
    ys = [yh, 1 - yh]

    arrived(seen.at[1 - s, dp], side_id)
    block_a()
    block_b()

    seen5 = seen
    arrived(seen5.at[0, slot(x, ys[1], z)], y_id)

    def pair_ref(nx, nz):
        return seen8.at[nx, :, nz]

    seen8 = seen.at[0].reshape(4, 2, 8, 3, 16, HS)
    for d in range(1, 8):
        send(pair_ref(x, z), pair_ref(x, z), dev(dz=d), za_id + d)
    for j in range(1, 4):
        send(pair_ref(x, z), pair_ref(x, z), dev(dx=j), xa_id + j - 1)

    for k, (dx, dy) in enumerate(plane[1:]):
        arrived(seen.at[1, slot(lax.rem(x + 4 - dx, 4), lax.rem(yh + dy, 2), z)], xyb_id + k)
    seenz = seen.at[1].reshape(8, 8, 3, 16, HS)

    def ring(step, towards):
        src = lax.rem(z + 8 - towards * (step - 1), 8)
        if step == 4:
            return seenz.at[pl.ds(0 if towards > 0 else 4, 4), src]
        return seenz.at[:, src]

    def ring_in(step, towards):
        src = lax.rem(z + 8 - towards * step, 8)
        if step == 4:
            return seenz.at[pl.ds(0 if towards > 0 else 4, 4), src]
        return seenz.at[:, src]

    def ring_id(step, towards):
        return zb_id + step * 2 + (0 if towards > 0 else 1)

    for t in (1, -1):
        send(ring(1, t), ring(1, t), dev(dz=t), ring_id(0, t))

    a_order = [1, 7, 2, 6, 3, 5, 4]
    plan = {1: a_order[:2], 2: a_order[2:4], 3: a_order[4:6], 4: a_order[6:]}
    for step in range(1, 5):
        for d in plan[step]:
            nz = lax.rem(z + 8 - d, 8)
            arrived(pair_ref(x, nz), za_id + d)
            for j in range(1, 4):
                send(pair_ref(x, nz), pair_ref(x, nz), dev(dx=j), xa_id + 3 * d + j - 1)
        for t in (1, -1):
            arrived(ring_in(step, t), ring_id(step - 1, t))
            if step < 4:
                send(ring(step + 1, t), ring(step + 1, t), dev(dz=t), ring_id(step, t))

    loads[0].wait()

    def project(m):
        wide[...] = seen[m].reshape(64 * 3 * 16, HS).astype(F32)
        total = jnp.zeros((192, 256), F32)
        for g in range(8):
            left_half = wide[pl.ds(2 * g, 192, stride=16), :]
            right_half = wide[pl.ds(2 * g + 1, 192, stride=16), :]
            piece = jnp.concatenate([left_half, right_half], axis=1).astype(BF)
            total = total + jnp.dot(piece, wo[256 * g : 256 * g + 256, :], preferred_element_type=F32)
        for k in range(2):
            part[2 * m + k] = total[96 * k : 96 * k + 96]
            part_bf[2 * m + k] = total[96 * k : 96 * k + 96].astype(BF)

    project(1)
    for d in range(8):
        nz = lax.rem(z + 8 - d, 8)
        for j in range(1, 4):
            arrived(pair_ref(lax.rem(x + 4 - j, 4), nz), xa_id + 3 * d + j - 1)
    project(0)

    group = [(1, 0), (0, 1), (1, 1)]
    q1 = ids(3)
    for k, (dh, ds) in enumerate(group):
        there = 2 * lax.rem(s + ds, 2) + lax.rem(h + dh, 2)
        send(part_bf.at[there], quarter_in.at[k], dev(dh=dh, ds=ds), q1 + k)
    total = res[mine].astype(F32) + part[mine]
    for k in range(3):
        arrived(quarter_in.at[k], q1 + k)
        total = total + quarter_in[k].astype(F32)
    hidden[...] = total
    scaled[mine] = (total * gain[...].astype(F32)).astype(BF)
    q2 = ids(3)
    for k, (dh, ds) in enumerate(group):
        send(scaled.at[mine], scaled.at[mine], dev(dh=dh, ds=ds), q2 + k)

    row_square = jnp.sum(total * total, axis=1, keepdims=True)
    diagonal = lax.broadcasted_iota(jnp.int32, (96, 128), 0) == lax.broadcasted_iota(jnp.int32, (96, 128), 1)
    lanes = jnp.sum(jnp.where(diagonal, row_square, 0.0), axis=0, keepdims=True)
    squares[0] = jnp.broadcast_to(lanes, (8, 128))
    sx, sy, sz, sq = ids(3), ids(1), ids(7), ids(3)
    for j in range(1, 4):
        send(squares.at[0], squares_in.at[j - 1], dev(dx=j), sx + j - 1)

    def squares_x():
        for j in range(3):
            arrived(squares_in.at[j], sx + j)
        squares[1] = squares[0] + squares_in[0] + squares_in[1] + squares_in[2]
        send(squares.at[1], squares_in.at[3], dev(dy=1), sy)

    def squares_y():
        arrived(squares_in.at[3], sy)
        squares[2] = squares[1] + squares_in[3]
        for d in range(1, 8):
            send(squares.at[2], squares_in.at[3 + d], dev(dz=d), sz + d - 1)

    def squares_z():
        value = squares[2]
        for d in range(1, 8):
            arrived(squares_in.at[3 + d], sz + d - 1)
            value = value + squares_in[3 + d]
        squares_all[mine] = value
        for k, (dh, ds) in enumerate(group):
            send(squares_all.at[mine], squares_all.at[mine], dev(dh=dh, ds=ds), sq + k)

    def squares_done():
        for k, (dh, ds) in enumerate(group):
            arrived(squares_all.at[2 * lax.rem(s + ds, 2) + lax.rem(h + dh, 2)], sq + k)

    for k, (dh, ds) in enumerate(group):
        arrived(scaled.at[2 * lax.rem(s + ds, 2) + lax.rem(h + dh, 2)], q2 + k)

    rows = scaled[...].reshape(384, 256)
    loads[1].wait()
    loads[2].wait()
    xa1, xa2, xa3 = ids(4), ids(4), ids(4)
    zb = ids(16)
    ya_id, zra = ids(2), ids(14)
    xyr = ids(14)
    weight = (wg, wu)
    back = [lax.rem(x + 4 - d, 4) for d in range(4)]

    def multiply_a(u):
        for p in range(NA):
            value = jnp.dot(rows, weight[u][:, 256 * p : 256 * p + 256], preferred_element_type=F32)
            pa[u, :, :, p] = value.astype(BF).reshape(4, 2, 48, 256)
        send(pa.at[u, xs[2], 0], pa_in1.at[u, 0], dev(dx=1), xa1 + 2 * u)
        send(pa.at[u, xs[2], 1], pa_in1.at[u, 1], dev(dx=-1), xa1 + 2 * u + 1)
        send(pa.at[u, xs[1], 1], pa_in2.at[u, 0, 1], dev(dx=1), xa2 + 2 * u)
        send(pa.at[u, xs[3], 0], pa_in2.at[u, 1, 0], dev(dx=-1), xa2 + 2 * u + 1)

    def z_block(u, dist, towards):
        there = lax.rem(z + 8 + towards * dist, 8)
        if dist == 4:
            return pb.at[u, there, pl.ds(0 if towards > 0 else 3, 3)]
        return pb.at[u, there]

    def z_in(u, dist, towards):
        dst = pb_in.at[u, 0 if towards > 0 else 1, dist - 1]
        if dist == 4:
            return dst.at[pl.ds(0 if towards > 0 else 3, 3)]
        return dst

    def z_id(u, dist, towards):
        return zb + 8 * u + 2 * (dist - 1) + (0 if towards > 0 else 1)

    def z_send(u, dist):
        for t in (1, -1):
            send(z_block(u, dist, t), z_in(u, dist, t), dev(dz=t), z_id(u, dist, t))

    def multiply_b(u):
        for p in range(NB):
            c = NA + p
            value = jnp.dot(rows, weight[u][:, 256 * c : 256 * c + 256], preferred_element_type=F32)
            pb[u, :, p] = value.astype(BF).reshape(8, 48, 256)
        z_send(u, 4)

    def z_step(u, dist):
        for t in (1, -1):
            arrived(z_in(u, dist, t), z_id(u, dist, t))
            there = lax.rem(z + 8 + t * (dist - 1), 8)
            d = 0 if t > 0 else 1
            if dist == 4:
                lo = 0 if t > 0 else 3
                pb[u, there, lo : lo + 3] = (
                    pb[u, there, lo : lo + 3].astype(F32) + pb_in[u, d, 3, lo : lo + 3].astype(F32)
                ).astype(BF)
            else:
                pb[u, there] = (pb[u, there].astype(F32) + pb_in[u, d, dist - 1].astype(F32)).astype(BF)
        z_send(u, dist - 1)

    def x_step(u):
        arrived(pa_in1.at[u, 0], xa1 + 2 * u)
        pa[u, xs[1], 0] = (pa[u, xs[1], 0].astype(F32) + pa_in1[u, 0].astype(F32)).astype(BF)
        send(pa.at[u, xs[1], 0], pa_in2.at[u, 0, 0], dev(dx=1), xa3 + 2 * u)
        arrived(pa_in1.at[u, 1], xa1 + 2 * u + 1)
        pa[u, xs[3], 1] = (pa[u, xs[3], 1].astype(F32) + pa_in1[u, 1].astype(F32)).astype(BF)
        send(pa.at[u, xs[3], 1], pa_in2.at[u, 1, 1], dev(dx=-1), xa3 + 2 * u + 1)

    def x_sum(u, ny):
        return pa[u, x, ny].astype(F32) + pa_in2[u, 0, ny].astype(F32) + pa_in2[u, 1, ny].astype(F32)

    def x_done(u):
        arrived(pa_in2.at[u, 0, 1], xa2 + 2 * u)
        arrived(pa_in2.at[u, 1, 0], xa2 + 2 * u + 1)
        arrived(pa_in2.at[u, 0, 0], xa3 + 2 * u)
        arrived(pa_in2.at[u, 1, 1], xa3 + 2 * u + 1)
        ya[u] = x_sum(u, ys[1]).astype(BF)
        send(ya.at[u], ya_in.at[u], dev(dy=1), ya_id + u)

    def y_done(u):
        arrived(ya_in.at[u], ya_id + u)
        za[u] = (x_sum(u, yh) + ya_in[u].astype(F32)).astype(BF)
        for d in range(1, 8):
            there = zs[d]

            @pl.when(there < NA)
            def _():
                send(za.at[u, there], za_in.at[u, d - 1], dev(dz=d), zra + 7 * u + d - 1, keep=False)

    def xb_start(u):
        for t in (1, -1):
            arrived(z_in(u, 1, t), z_id(u, 1, t))
        xb[u] = (
            pb[u, z].astype(F32) + pb_in[u, 0, 0].astype(F32) + pb_in[u, 1, 0].astype(F32)
        ).astype(BF)
        for k, (dx, dy) in enumerate(plane[1:]):
            there = 2 * xs[dx] + ys[dy]

            @pl.when(there < NB)
            def _():
                send(xb.at[u, there], xb_in.at[u, k], dev(dx=dx, dy=dy), xyr + 7 * u + k, keep=False)

    for u in range(2):
        multiply_a(u)
        multiply_b(u)
    squares_x()
    for u in range(2):
        z_step(u, 4)
        x_step(u)
    squares_y()
    z_step(0, 3)
    z_step(1, 3)
    squares_z()
    x_done(0)
    z_step(0, 2)
    y_done(0)
    z_step(1, 2)
    squares_done()
    x_done(1)
    xb_start(0)
    y_done(1)
    xb_start(1)

    def scaling(index, offset):
        lane_scale = lax.rsqrt(squares_all[index][:1] / D + 1e-05)
        pick = (
            lax.broadcasted_iota(jnp.int32, (48, 128), 0) + offset
            == lax.broadcasted_iota(jnp.int32, (48, 128), 1)
        )
        return jnp.sum(jnp.where(pick, lane_scale, 0.0), axis=1, keepdims=True)

    def activate(gate, upper, scale):
        gate = gate * scale
        return (gate / (1.0 + jnp.exp(-gate)) * (upper * scale)).astype(BF)

    ga, gay, gax = ids(8), ids(8), ids(42)
    gb, gbz = ids(8), ids(16)

    @pl.when(z < NA)
    def _():
        sums = []
        for u in range(2):
            value = za[u, lax.rem(z, NA)].astype(F32)
            for d in range(1, 8):
                arrived(za_in.at[u, d - 1], zra + 7 * u + d - 1)
                value = value + za_in[u, d - 1].astype(F32)
            sums.append(value)
        act_a[xy, z] = activate(sums[0], sums[1], scaling(x, 48 * yh))
        for d in range(1, 8):
            send(act_a.at[xy, z], act_a.at[xy, z], dev(dz=d), ga + d, keep=False)

    @pl.when(xy < NB)
    def _():
        sums = []
        for u in range(2):
            value = xb[u, xy].astype(F32)
            for k in range(7):
                arrived(xb_in.at[u, k], xyr + 7 * u + k)
                value = value + xb_in[u, k].astype(F32)
            sums.append(value)
        act_b[z, xy] = activate(sums[0], sums[1], scaling(z // 2, 48 * lax.rem(z, 2)))
        for k, (dx, dy) in enumerate(plane[1:]):
            send(act_b.at[z, xy], act_b.at[z, xy], dev(dx=dx, dy=dy), gb + k, keep=False)

    for k, (dx, dy) in enumerate(plane[1:]):
        there = 2 * back[dx] + ys[dy]

        @pl.when(there < NB)
        def _():
            arrived(act_b.at[z, there], gb + k)

    def gz(step, towards, shift):
        src = lax.rem(z + 8 - towards * (step - 1 + shift), 8)
        if step == 4:
            return act_b.at[src, pl.ds(0 if towards > 0 else 3, 3)]
        return act_b.at[src]

    def gz_id(step, towards):
        return gbz + 2 * step + (0 if towards > 0 else 1)

    for t in (1, -1):
        send(gz(1, t, 0), gz(1, t, 0), dev(dz=t), gz_id(0, t))

    order = [0, 1, 7, 2, 6, 3, 5, 4]

    def a_ref(nx, ny, nz):
        return act_a.at[2 * nx + ny, nz]

    def a_step(d):
        nz = lax.rem(z + 8 - d, 8)

        @pl.when(nz < NA)
        def _():
            if d > 0:
                arrived(a_ref(x, yh, nz), ga + d)
            send(a_ref(x, yh, nz), a_ref(x, yh, nz), dev(dy=1), gay + d, keep=False)

    def pair_a(nx, nz):
        return act_a.at[pl.ds(2 * nx, 2), nz]

    def a_step2(d):
        nz = lax.rem(z + 8 - d, 8)

        @pl.when(nz < NA)
        def _():
            arrived(a_ref(x, ys[1], nz), gay + d)
            for j in range(1, 4):
                send(pair_a(x, nz), pair_a(x, nz), dev(dx=j), gax + 3 * d + j - 1 if d < 8 else 0, keep=False)

    a_step(0)
    a_step(1)
    a_step(7)
    a_step2(0)
    a_step(2)
    a_step(6)
    a_step2(1)
    a_step2(7)
    for step in range(1, 5):
        for t in (1, -1):
            arrived(gz(step, t, 1), gz_id(step - 1, t))
            if step < 4:
                send(gz(step + 1, t, 0), gz(step + 1, t, 0), dev(dz=t), gz_id(step, t))
        if step == 1:
            a_step(3)
            a_step(5)
            a_step(4)
            a_step2(2)
            a_step2(6)
        if step == 2:
            a_step2(3)
            a_step2(5)
            a_step2(4)

    loads[3].wait()
    value = jnp.zeros((384, 256), F32)
    for p in range(NB):
        block = act_b[:, p].reshape(384, 256)
        value = value + jnp.dot(block, wd[256 * (NA + p) : 256 * (NA + p) + 256, :], preferred_element_type=F32)
    down[...] = value.reshape(4, 96, 256)
    for d in range(8):
        nz = lax.rem(z + 8 - d, 8)

        @pl.when(nz < NA)
        def _():
            for j in range(1, 4):
                arrived(pair_a(back[j], nz), gax + 3 * d + j - 1)

    value = down[...].reshape(384, 256)
    for p in range(NA):
        block = act_a[:, p].reshape(384, 256)
        value = value + jnp.dot(block, wd[256 * p : 256 * p + 256, :], preferred_element_type=F32)
    down[...] = value.reshape(4, 96, 256)
    down_bf[...] = value.astype(BF).reshape(4, 96, 256)

    q3 = ids(3)
    for k, (dh, ds) in enumerate(group):
        there = 2 * lax.rem(s + ds, 2) + lax.rem(h + dh, 2)
        send(down_bf.at[there], down_in.at[k], dev(dh=dh, ds=ds), q3 + k)
    total = hidden[...] + down[mine]
    for k in range(3):
        arrived(down_in.at[k], q3 + k)
        total = total + down_in[k].astype(F32)
    fin[0] = total[:, :128]
    fin[1] = total[:, 128:]

    for r in range(3):
        for j in range(2):
            send1[pl.ds(2 * r + j, 32, stride=8), :] = fin[j, pl.ds(r, 32, stride=3), :]
    for j in range(2):
        send1[pl.ds(6 + j, 32, stride=8), :] = jnp.zeros((32, 128), F32)
    blocks = send1.reshape(4, 8, 8, 128)
    f1 = ids(7)
    for d in range(1, 8):
        send(blocks.at[:, zs[d]], mid.at[z], dev(dz=d), f1 + d - 1)
    mid[z] = blocks[:, z]
    for d in range(1, 8):
        arrived(mid.at[lax.rem(z + 8 - d, 8)], f1 + d - 1)

    f2 = ids(16)
    targets = []
    for xl in range(2):
        for ny in range(2):
            for nh in range(2):
                nx = 2 * h + xl
                own = (nx == x) & (ny == yh) & (nh == h)
                index = 4 * xl + 2 * ny + nh
                targets.append((2 * xl + ny, own, index))

                @pl.when(own)
                def _():
                    out[xy] = mid[:, 2 * xl + ny]

                @pl.when(jnp.logical_not(own))
                def _():
                    copy = pltpu.make_async_remote_copy(
                        src_ref=mid.at[:, 2 * xl + ny], dst_ref=out.at[xy], send_sem=ss.at[f2 + index],
                        recv_sem=rs.at[f2 + xy], device_id=((nx * 2 + ny) * 8 + z, nh, s), device_id_type=MESH,
                    )
                    copy.start()
    for k in range(8):
        own = (xy == k) & (h == x // 2)

        @pl.when(jnp.logical_not(own))
        def _():
            arrived(out.at[k], f2 + k)

    for block, own, index in targets:
        @pl.when(jnp.logical_not(own))
        def _():
            left(mid.at[:, block], f2 + index)
    for copy in pending:
        copy.wait_send()
    for d in range(1, 8):
        @pl.when(zs[d] < NA)
        def _():
            for u in range(2):
                left(za.at[u, 0], zra + 7 * u + d - 1)
    for k, (dx, dy) in enumerate(plane[1:]):
        @pl.when(2 * xs[dx] + ys[dy] < NB)
        def _():
            for u in range(2):
                left(xb.at[u, 0], xyr + 7 * u + k)

    @pl.when(z < NA)
    def _():
        for d in range(1, 8):
            left(act_a.at[0, 0], ga + d)

    @pl.when(xy < NB)
    def _():
        for k in range(7):
            left(act_b.at[0, 0], gb + k)

    for d in range(8):
        @pl.when(lax.rem(z + 8 - d, 8) < NA)
        def _():
            left(act_a.at[0, 0], gay + d)
            for j in range(1, 4):
                left(act_a.at[pl.ds(0, 2), 0], gax + 3 * d + j - 1)
    assert counter[0] <= SEMS


SEMS = 320


def slab(att, residual, gain, out_weight, gate_weight, up_weight, down_weight):
    vmem = pl.BlockSpec(memory_space=pltpu.VMEM)
    anywhere = pl.BlockSpec(memory_space=pl.ANY)
    scratch = [
        pltpu.VMEM((2048, 256), BF),
        pltpu.VMEM((256, 3328), BF),
        pltpu.VMEM((256, 3328), BF),
        pltpu.VMEM((3328, 256), BF),
        pltpu.VMEM((2, 64, 3, 16, HS), BF),
        pltpu.VMEM((64 * 3 * 16, HS), F32),
        pltpu.VMEM((4, 96, 256), F32),
        pltpu.VMEM((4, 96, 256), BF),
        pltpu.VMEM((3, 96, 256), BF),
        pltpu.VMEM((96, 256), F32),
        pltpu.VMEM((4, 96, 256), BF),
        pltpu.VMEM((3, 8, 128), F32),
        pltpu.VMEM((11, 8, 128), F32),
        pltpu.VMEM((4, 8, 128), F32),
        pltpu.VMEM((2, 4, 2, NA, 48, 256), BF),
        pltpu.VMEM((2, 2, NA, 48, 256), BF),
        pltpu.VMEM((2, 2, 2, NA, 48, 256), BF),
        pltpu.VMEM((2, NA, 48, 256), BF),
        pltpu.VMEM((2, NA, 48, 256), BF),
        pltpu.VMEM((2, NA, 48, 256), BF),
        pltpu.VMEM((2, 7, 48, 256), BF),
        pltpu.VMEM((2, 8, NB, 48, 256), BF),
        pltpu.VMEM((2, 2, 4, NB, 48, 256), BF),
        pltpu.VMEM((2, NB, 48, 256), BF),
        pltpu.VMEM((2, 7, 48, 256), BF),
        pltpu.VMEM((8, NA, 48, 256), BF),
        pltpu.VMEM((8, NB, 48, 256), BF),
        pltpu.VMEM((4, 96, 256), F32),
        pltpu.VMEM((4, 96, 256), BF),
        pltpu.VMEM((3, 96, 256), BF),
        pltpu.VMEM((2, 96, 128), F32),
        pltpu.VMEM((256, 128), F32),
        pltpu.VMEM((8, 4, 8, 128), F32),
        pltpu.SemaphoreType.DMA((4,)),
        pltpu.SemaphoreType.DMA((SEMS,)),
        pltpu.SemaphoreType.DMA((SEMS,)),
    ]
    return pl.pallas_call(
        slab_kernel,
        out_shape=jax.ShapeDtypeStruct((8, 8, 8, 128), F32),
        in_specs=[vmem, vmem, vmem, anywhere, anywhere, anywhere, anywhere],
        out_specs=vmem,
        scratch_shapes=scratch,
        compiler_params=pltpu.CompilerParams(collective_id=0, has_side_effects=True, vmem_limit_bytes=VMEM_LIMIT),
        cost_estimate=pl.CostEstimate(flops=2 * 384 * 256 * 12032, bytes_accessed=8 * 2**20, transcendentals=0),
        name="slab",
    )(att, residual.reshape(4, 96, 256), gain.reshape(1, 256), out_weight, gate_weight, up_weight, down_weight)


def body(
    queries,
    new_keys,
    new_values,
    key_cache,
    value_cache,
    cache_lengths,
    residual,
    norm_gain,
    out_weight,
    gate_weight,
    up_weight,
    down_weight,
):
    attended = attend(queries, new_keys, new_values, key_cache, value_cache, cache_lengths)
    rows = slab(attended, residual, norm_gain, out_weight, gate_weight, up_weight, down_weight)
    rows = rows.reshape(64, 8, HS)[:, :6].reshape(64, 3, 2 * HS)
    return rows.transpose(1, 0, 2).reshape(1, 3, D).astype(BF)


def solution(mesh):
    return jax.shard_map(
        body,
        mesh=mesh,
        in_specs=(
            P("side", "dp", "head"),
            P("side", "dp", "head"),
            P("side", "dp", "head"),
            P("side", "dp", None, "head"),
            P("side", "dp", None, "head"),
            P("side", "dp"),
            P(None, None, "dp"),
            P("dp"),
            P(("head", "side"), "dp"),
            P("dp", ("head", "side")),
            P("dp", ("head", "side")),
            P(("head", "side"), "dp"),
        ),
        out_specs=P("side", "dp", None),
        check_vma=False,
    )
```

```python
import math

import jax
import jax.numpy as jnp
from jax import lax
from jax.experimental import pallas as pl
from jax.experimental.pallas import tpu as pltpu
from jax.sharding import PartitionSpec as P

D = 16384
HS = 128
BF = jnp.bfloat16
F32 = jnp.float32
MESH = pl.DeviceIdType.MESH
VMEM_LIMIT = 56 * 2**20

UNITS = 1664
NA = 8
NB = 5
PUSH = (1, 5, 2)
FLAT = 256


def attend_row(length, q, new_key, new_value, keys, values):
    span = keys.shape[0]
    zero = jnp.zeros((16, HS), F32)
    wide = jnp.concatenate(
        [jnp.concatenate([q[:16], zero], axis=1), jnp.concatenate([zero, q[16:]], axis=1)], axis=0
    )
    scale = 1.0 / math.sqrt(HS)
    nt = (((1,), (1,)), ((), ()))
    scores = lax.dot_general(wide.astype(BF), keys, nt, preferred_element_type=F32) * scale
    fresh = jnp.sum(wide * new_key, axis=1, keepdims=True) * scale
    valid = lax.broadcasted_iota(jnp.int32, (32, span), 1) < length
    masked = jnp.where(valid, scores, -jnp.inf)
    highest = jnp.maximum(jnp.max(masked, axis=1, keepdims=True), fresh)
    probs = jnp.exp(masked - highest)
    fresh_prob = jnp.exp(fresh - highest)
    total = jnp.sum(probs, axis=1, keepdims=True) + fresh_prob
    inverse = 1.0 / total
    weights = (probs * inverse).astype(BF)
    fresh_weight = (fresh_prob * inverse).astype(BF).astype(F32)
    mixed = jnp.dot(weights, values, preferred_element_type=F32) + fresh_weight * new_value
    return mixed[:16, :HS].astype(BF), mixed[16:, HS:].astype(BF)


def layer_kernel(
    lengths, queries, new_keys, new_values, key_hbm, value_hbm,
    res, gain, wo_hbm, wg_hbm, wu_hbm, wd_hbm,
    out,
    keys, values, att, wo, wg, wu, wd,
    seen, wide, part, part_bf, quarter_in, hidden, scaled,
    squares_mine, squares, squares_in, squares_all,
    pa, pa_in1, pa_in2, za, za_in,
    pb, pb_in, xb, xb_in, scale_rows,
    act_a, act_b, down, down_bf, down_in, fin, send1, mid,
    csem, wsem, ss, rs,
):
    dp = lax.axis_index("dp")
    h = lax.axis_index("head")
    s = lax.axis_index("side")
    z = lax.rem(dp, 8)
    xy = dp // 8
    yh = lax.rem(xy, 2)
    x = xy // 2
    mine = 2 * s + h

    def dev(dx=0, dy=0, dz=0, dh=0, ds=0):
        nx = lax.rem(x + (dx + 4), 4)
        ny = lax.rem(yh + dy, 2)
        nz = lax.rem(z + (dz + 8), 8)
        return ((nx * 2 + ny) * 8 + nz, lax.rem(h + dh, 2), lax.rem(s + ds, 2))

    counter = [0]
    pending = []

    def ids(count):
        first = counter[0]
        counter[0] += count
        return first

    def when(condition, action):
        if condition is None:
            action()
        else:
            pl.when(condition)(action)

    def copy_of(src, dst, target, send_index, recv_index):
        return pltpu.make_async_remote_copy(
            src_ref=src, dst_ref=dst, send_sem=ss.at[send_index], recv_sem=rs.at[recv_index],
            device_id=target, device_id_type=MESH,
        )

    def send(src, dst, target, index, condition=None, slot=None):
        when(condition, copy_of(src, dst, target, index, index if slot is None else slot).start)
        pending.append((src, index, condition))

    def arrived(ref, index):
        copy_of(ref, ref, dev(dh=1), index, index).wait_recv()

    caches = []
    for r in range(3):
        for k, (src, dst) in enumerate(((key_hbm, keys), (value_hbm, values))):
            copy = pltpu.make_async_copy(src.at[r], dst.at[r], csem.at[2 * r + k])
            copy.start()
            caches.append(copy)

    plane = [(dx, dy) for dx in range(4) for dy in range(2)]
    peers = [dict(dx=dx, dy=dy, dh=dh) for dx, dy in plane for dh in range(2) if dx or dy or dh]
    peers += [dict(dz=dz) for dz in range(1, 8)]
    peers += [dict(dy=dy, dh=dh, ds=1) for dy in range(2) for dh in range(2)]
    barrier = pltpu.get_barrier_semaphore()
    for peer in peers:
        pl.semaphore_signal(barrier, inc=1, device_id=dev(**peer), device_id_type=MESH)

    loads = []

    def load(src, dst):
        copy = pltpu.make_async_copy(src, dst, wsem.at[len(loads)])
        copy.start()
        loads.append(copy)

    units = pl.ds(pl.multiple_of(UNITS * yh, 128), UNITS)
    others = pl.ds(pl.multiple_of(UNITS * (1 - yh), 128), UNITS)
    w_id = ids(9)
    pieces = [
        (src.at[pl.ds(64 * k, 64), others], dst.at[yh, pl.ds(64 * k, 64)])
        for src, dst in ((wg_hbm, wg), (wu_hbm, wu)) for k in range(4)
    ]
    pushed = [0]

    def push(count):
        for _ in range(count):
            src, dst = pieces[pushed[0]]
            send(src, dst, dev(dy=1), w_id + pushed[0])
            pushed[0] += 1

    for r in range(3):
        q = queries[...].astype(F32)[r : r + 1]
        q = jnp.concatenate([q[:, HS * g : HS * g + HS] for g in range(32)], axis=0)
        caches[2 * r].wait()
        caches[2 * r + 1].wait()
        if r == 2:
            load(wo_hbm, wo)
            load(wg_hbm.at[:, units], wg.at[yh])
            load(wu_hbm.at[:, units], wu.at[yh])
            load(wd_hbm.at[units], wd.at[yh])
        low, high = attend_row(
            lengths[0, r], q, new_keys[...].astype(F32)[r : r + 1], new_values[...].astype(F32)[r : r + 1],
            keys[r], values[r],
        )
        att[r, 0] = low
        att[r, 1] = high
        if r == 0:
            pl.semaphore_wait(barrier, len(peers))
            push(PUSH[0])

    y_id = ids(4)
    for ny in range(2):
        for ns in range(2):
            if ny or ns:
                head = s if ns == 0 else 1 - s
                send(att.at[:, head], seen.at[s, dp], dev(dy=ny, ds=ns), y_id + 2 * ny + ns)
    seen[s, dp] = att[:, s]

    za_id = ids(8)
    xa_id = ids(8 * 3)
    xyb_id = ids(8)
    zb_id = ids(16)

    def slot(nx, ny, nz):
        return (nx * 2 + ny) * 8 + nz

    xs = [lax.rem(x + d, 4) for d in range(4)]
    zs = [lax.rem(z + d, 8) for d in range(8)]
    ys = [yh, 1 - yh]

    arrived(seen.at[1 - s, dp], y_id + 1)
    there = slot(x, ys[1], z)
    arrived(seen.at[s, there], y_id + 2)
    arrived(seen.at[1 - s, there], y_id + 3)

    push(PUSH[1])

    seen8 = seen.at[0].reshape(4, 2, 8, 3, 16, HS)

    def pair_ref(nx, nz):
        return seen8.at[nx, :, nz]

    for d in range(1, 8):
        send(pair_ref(x, z), pair_ref(x, z), dev(dz=d), za_id + d)
    for j in range(1, 4):
        send(pair_ref(x, z), pair_ref(x, z), dev(dx=j), xa_id + j - 1)

    seenx = seen.at[1].reshape(4, 2, 8, 3, 16, HS)
    for j in range(1, 4):
        send(seenx.at[x, :, z], seenx.at[x, :, z], dev(dx=j), xyb_id + j)
    for j in range(1, 4):
        arrived(seenx.at[lax.rem(x + 4 - j, 4), :, z], xyb_id + j)
    seenz = seen.at[1].reshape(8, 8, 3, 16, HS)

    def ring(step, towards):
        src = lax.rem(z + 8 - towards * (step - 1), 8)
        if step == 4:
            return seenz.at[pl.ds(0 if towards > 0 else 4, 4), src]
        return seenz.at[:, src]

    def ring_in(step, towards):
        src = lax.rem(z + 8 - towards * step, 8)
        if step == 4:
            return seenz.at[pl.ds(0 if towards > 0 else 4, 4), src]
        return seenz.at[:, src]

    def ring_id(step, towards):
        return zb_id + step * 2 + (0 if towards > 0 else 1)

    for t in (1, -1):
        send(ring(1, t), ring(1, t), dev(dz=t), ring_id(0, t))

    a_order = [1, 7, 2, 6, 3, 5, 4]
    plan = {1: a_order[:2], 2: a_order[2:4], 3: a_order[4:6], 4: a_order[6:]}
    for step in range(1, 5):
        for d in plan[step]:
            nz = lax.rem(z + 8 - d, 8)
            arrived(pair_ref(x, nz), za_id + d)
            for j in range(1, 4):
                send(pair_ref(x, nz), pair_ref(x, nz), dev(dx=j), xa_id + 3 * d + j - 1)
        for t in (1, -1):
            arrived(ring_in(step, t), ring_id(step - 1, t))
            if step < 4:
                send(ring(step + 1, t), ring(step + 1, t), dev(dz=t), ring_id(step, t))

    loads[0].wait()

    def project(m):
        wide[...] = seen[m].reshape(64 * 3 * 16, HS).astype(F32)
        total = jnp.zeros((192, 256), F32)
        for g in range(8):
            left_half = wide[pl.ds(2 * g, 192, stride=16), :]
            right_half = wide[pl.ds(2 * g + 1, 192, stride=16), :]
            piece = jnp.concatenate([left_half, right_half], axis=1).astype(BF)
            total = total + jnp.dot(piece, wo[256 * g : 256 * g + 256, :], preferred_element_type=F32)
        for k in range(2):
            part[2 * m + k] = total[96 * k : 96 * k + 96]
            part_bf[2 * m + k] = total[96 * k : 96 * k + 96].astype(BF)

    project(1)
    for d in range(8):
        nz = lax.rem(z + 8 - d, 8)
        for j in range(1, 4):
            arrived(pair_ref(lax.rem(x + 4 - j, 4), nz), xa_id + 3 * d + j - 1)
    project(0)

    group = [(1, 0), (0, 1), (1, 1)]
    q1 = ids(3)
    for k, (dh, ds) in enumerate(group):
        there = 2 * lax.rem(s + ds, 2) + lax.rem(h + dh, 2)
        send(part_bf.at[there], quarter_in.at[k], dev(dh=dh, ds=ds), q1 + k)
    total = res[mine].astype(F32) + part[mine]
    for k in range(3):
        arrived(quarter_in.at[k], q1 + k)
        total = total + quarter_in[k].astype(F32)
    hidden[...] = total
    scaled[yh, mine] = (total * gain[...].reshape(1, 256).astype(F32)).astype(BF)
    group8 = [(dy, dh, ds) for dy in range(2) for dh in range(2) for ds in range(2)][1:]
    q2 = ids(7)

    def quarter(dh, ds):
        return 2 * lax.rem(s + ds, 2) + lax.rem(h + dh, 2)

    for k, (dy, dh, ds) in enumerate(group8):
        send(scaled.at[yh, mine], scaled.at[yh, mine], dev(dy=dy, dh=dh, ds=ds), q2 + k)

    row_square = jnp.sum(total * total, axis=1, keepdims=True)
    diagonal = lax.broadcasted_iota(jnp.int32, (96, 128), 0) == lax.broadcasted_iota(jnp.int32, (96, 128), 1)
    lanes = jnp.sum(jnp.where(diagonal, row_square, 0.0), axis=0, keepdims=True)
    squares_mine[yh, mine] = jnp.broadcast_to(lanes, (8, 128))
    sg, sx, sz = ids(7), ids(3), ids(7)
    for k, (dy, dh, ds) in enumerate(group8):
        send(squares_mine.at[yh, mine], squares_mine.at[yh, mine], dev(dy=dy, dh=dh, ds=ds), sg + k)

    def squares_x():
        for k, (dy, dh, ds) in enumerate(group8):
            arrived(squares_mine.at[ys[dy], quarter(dh, ds)], sg + k)
        row = lax.broadcasted_iota(jnp.int32, (8, 128), 0)
        value = jnp.zeros((8, 128), F32)
        for k in range(4):
            value = value + jnp.where(row == k, squares_mine[0, k] + squares_mine[1, k], 0.0)
        squares[0] = value
        for j in range(1, 4):
            send(squares.at[0], squares_in.at[j - 1], dev(dx=j), sx + j - 1)

    def squares_z():
        for j in range(3):
            arrived(squares_in.at[j], sx + j)
        squares[1] = squares[0] + squares_in[0] + squares_in[1] + squares_in[2]
        for d in range(1, 8):
            send(squares.at[1], squares_in.at[2 + d], dev(dz=d), sz + d - 1)

    def squares_done():
        value = squares[1]
        for d in range(1, 8):
            arrived(squares_in.at[2 + d], sz + d - 1)
            value = value + squares_in[2 + d]
        squares_all[...] = lax.rsqrt(value / D + 1e-05)

    push(PUSH[2])
    send(wd_hbm.at[others], wd.at[yh], dev(dy=1), w_id + 8)
    for k, (dy, dh, ds) in enumerate(group8):
        arrived(scaled.at[ys[dy], quarter(dh, ds)], q2 + k)

    rows = jnp.concatenate([scaled[0].reshape(384, 256), scaled[1].reshape(384, 256)], axis=1)
    xa1, xa2, xa3 = ids(4), ids(4), ids(4)
    zb = ids(16)
    zra = ids(14)
    xyr = ids(6)
    weight = (wg, wu)
    back = [lax.rem(x + 4 - d, 4) for d in range(4)]
    def multiply(u, c, count):
        columns = weight[u][:, :, 128 * c : 128 * (c + count)].reshape(512, 128 * count)
        value = jnp.dot(rows, columns, preferred_element_type=F32).astype(BF)
        return [value[:, 128 * i : 128 * i + 128] for i in range(count)]

    def multiply_a(u):
        for c in range(0, NA, 2):
            for i, value in enumerate(multiply(u, c, 2)):
                pa[u, :, :, c + i] = value.reshape(4, 2, 48, 128)
        send(pa.at[u, xs[2], 0], pa_in1.at[u, 0], dev(dx=1), xa1 + 2 * u)
        send(pa.at[u, xs[2], 1], pa_in1.at[u, 1], dev(dx=-1), xa1 + 2 * u + 1)
        send(pa.at[u, xs[1], 1], pa_in2.at[u, 0, 1], dev(dx=1), xa2 + 2 * u)
        send(pa.at[u, xs[3], 0], pa_in2.at[u, 1, 0], dev(dx=-1), xa2 + 2 * u + 1)

    def half(towards):
        return pl.ds(0 if towards > 0 else FLAT // 2, FLAT // 2)

    def z_block(u, dist, towards):
        there = lax.rem(z + 8 + towards * dist, 8)
        if dist == 4:
            return pb.at[u, there, half(towards)]
        return pb.at[u, there]

    def z_in(u, dist, towards):
        dst = pb_in.at[u, 0 if towards > 0 else 1, dist - 1]
        if dist == 4:
            return dst.at[half(towards)]
        return dst

    def z_id(u, dist, towards):
        return zb + 8 * u + 2 * (dist - 1) + (0 if towards > 0 else 1)

    def z_send(u, dist):
        for t in (1, -1):
            send(z_block(u, dist, t), z_in(u, dist, t), dev(dz=t), z_id(u, dist, t))

    def multiply_b(u):
        for c in range(0, NB, 2):
            for i, value in enumerate(multiply(u, NA + c, min(2, NB - c))):
                pb[u, :, 48 * (c + i) : 48 * (c + i) + 48] = value.reshape(8, 48, 128)
        pb[u, :, 48 * NB :] = jnp.zeros((8, FLAT - 48 * NB, 128), BF)
        z_send(u, 4)

    def z_step(u, dist):
        for t in (1, -1):
            arrived(z_in(u, dist, t), z_id(u, dist, t))
            there = lax.rem(z + 8 + t * (dist - 1), 8)
            d = 0 if t > 0 else 1
            part_rows = half(t) if dist == 4 else pl.ds(0, FLAT)
            pb[u, there, part_rows] = (
                pb[u, there, part_rows].astype(F32) + pb_in[u, d, dist - 1, part_rows].astype(F32)
            ).astype(BF)
        z_send(u, dist - 1)

    def x_step(u):
        arrived(pa_in1.at[u, 0], xa1 + 2 * u)
        pa[u, xs[1], 0] = (pa[u, xs[1], 0].astype(F32) + pa_in1[u, 0].astype(F32)).astype(BF)
        send(pa.at[u, xs[1], 0], pa_in2.at[u, 0, 0], dev(dx=1), xa3 + 2 * u)
        arrived(pa_in1.at[u, 1], xa1 + 2 * u + 1)
        pa[u, xs[3], 1] = (pa[u, xs[3], 1].astype(F32) + pa_in1[u, 1].astype(F32)).astype(BF)
        send(pa.at[u, xs[3], 1], pa_in2.at[u, 1, 1], dev(dx=-1), xa3 + 2 * u + 1)

    def x_done(u):
        arrived(pa_in2.at[u, 0, 1], xa2 + 2 * u)
        arrived(pa_in2.at[u, 1, 0], xa2 + 2 * u + 1)
        arrived(pa_in2.at[u, 0, 0], xa3 + 2 * u)
        arrived(pa_in2.at[u, 1, 1], xa3 + 2 * u + 1)
        for k in range(2):
            za[u, k] = (
                pa[u, x, k].astype(F32) + pa_in2[u, 0, k].astype(F32) + pa_in2[u, 1, k].astype(F32)
            ).astype(BF)
        for d in range(1, 8):
            send(za.at[u, :, zs[d]], za_in.at[u, d - 1], dev(dz=d), zra + 7 * u + d - 1)

    def own_flat(nx):
        return pl.ds(pl.multiple_of(FLAT // 4 * nx, FLAT // 4), FLAT // 4)

    def xb_start(u):
        for t in (1, -1):
            arrived(z_in(u, 1, t), z_id(u, 1, t))
        xb[u] = (
            pb[u, z].astype(F32) + pb_in[u, 0, 0].astype(F32) + pb_in[u, 1, 0].astype(F32)
        ).astype(BF)
        for j in range(1, 4):
            send(xb.at[u, own_flat(xs[j])], xb_in.at[u, j - 1], dev(dx=j), xyr + 3 * u + j - 1)

    squares_x()
    loads[1].wait()
    loads[2].wait()
    for u in range(2):
        for k in range(4):
            arrived(weight[u].at[1 - yh, pl.ds(64 * k, 64)], w_id + 4 * u + k)
        multiply_a(u)
        multiply_b(u)
    z_step(0, 4)
    x_step(0)
    z_step(1, 4)
    x_step(1)
    z_step(0, 3)
    z_step(1, 3)
    squares_z()
    x_done(0)
    z_step(0, 2)
    z_step(1, 2)
    x_done(1)
    squares_done()
    xb_start(0)
    xb_start(1)

    def scaling(index, offset, count):
        lane_scale = squares_all[pl.ds(index, 1)]
        pick = (
            lax.broadcasted_iota(jnp.int32, (count, 128), 0) + offset
            == lax.broadcasted_iota(jnp.int32, (count, 128), 1)
        )
        return jnp.sum(jnp.where(pick, lane_scale, 0.0), axis=1, keepdims=True)

    def activate(gate, upper, scale):
        gate = gate * scale
        return (gate / (1.0 + jnp.exp(-gate)) * (upper * scale)).astype(BF)

    ga, gax = ids(8), ids(24)
    gb, gbz = ids(4), ids(8)

    scale_rows[...] = jnp.broadcast_to(scaling(z // 2, 48 * lax.rem(z, 2), 48), (48, 128)).reshape(3, 16, 128)
    sums = []
    for u in range(2):
        value = xb[u, own_flat(x)].astype(F32)
        for j in range(3):
            arrived(xb_in.at[u, j], xyr + 3 * u + j)
            value = value + xb_in[u, j].astype(F32)
        sums.append(value)
    tiles = [scale_rows[lax.rem(4 * x + i, 3)] for i in range(4)]
    act_b[z, own_flat(x)] = activate(sums[0], sums[1], jnp.concatenate(tiles, axis=0))
    for j in range(1, 4):
        send(act_b.at[z, own_flat(x)], act_b.at[z, own_flat(x)], dev(dx=j), gb + j)

    sums = []
    for u in range(2):
        value = za[u, :, z].astype(F32)
        for d in range(1, 8):
            arrived(za_in.at[u, d - 1], zra + 7 * u + d - 1)
            value = value + za_in[u, d - 1].astype(F32)
        sums.append(value.reshape(96, 128))
    act_a[x, z] = activate(sums[0], sums[1], scaling(x, 0, 96))
    for d in range(1, 8):
        send(act_a.at[x, z], act_a.at[x, z], dev(dz=d), ga + d)
    for j in range(1, 4):
        send(act_a.at[x, z], act_a.at[x, z], dev(dx=j), gax + j - 1)

    for j in range(1, 4):
        arrived(act_b.at[z, own_flat(back[j])], gb + j)

    def gz(step, towards, shift):
        src = lax.rem(z + 8 - towards * (step - 1 + shift), 8)
        if step == 4:
            return act_b.at[src, half(towards)]
        return act_b.at[src]

    def gz_id(step, towards):
        return gbz + 2 * step + (0 if towards > 0 else 1)

    for t in (1, -1):
        send(gz(1, t, 0), gz(1, t, 0), dev(dz=t), gz_id(0, t))

    def a_step(d):
        nz = zs[(8 - d) % 8]
        arrived(act_a.at[x, nz], ga + d)
        for j in range(1, 4):
            send(act_a.at[x, nz], act_a.at[x, nz], dev(dx=j), gax + 3 * d + j - 1)

    for step in range(1, 5):
        for d in plan[step]:
            a_step(d)
        for t in (1, -1):
            arrived(gz(step, t, 1), gz_id(step - 1, t))
            if step < 4:
                send(gz(step + 1, t, 0), gz(step + 1, t, 0), dev(dz=t), gz_id(step, t))

    loads[3].wait()
    arrived(wd.at[1 - yh], w_id + 8)

    def lower(chunks, first):
        for i in range(0, len(chunks), 2):
            pieces, numbers = zip(*chunks[i : i + 2])
            piece = jnp.concatenate(pieces, axis=1) if len(pieces) == 2 else pieces[0]
            depth = pl.ds(128 * numbers[0], 128 * len(numbers))
            for ny in range(2):
                value = jnp.dot(piece, wd[ny, depth], preferred_element_type=F32).reshape(4, 96, 256)
                if first and i == 0:
                    down[ny] = value
                else:
                    down[ny] += value

    lower([(act_b[:, 48 * c : 48 * c + 48].reshape(384, 128), NA + c) for c in range(NB)], True)
    for d in range(8):
        for j in range(1, 4):
            arrived(act_a.at[back[j], zs[(8 - d) % 8]], gax + 3 * d + j - 1)
    lower([(act_a[:, c].reshape(384, 128), c) for c in range(NA)], False)
    down_bf[...] = down[...].astype(BF)

    q3 = ids(7)
    for k, (dy, dh, ds) in enumerate(group8):
        send(down_bf.at[ys[dy], quarter(dh, ds)], down_in.at[k], dev(dy=dy, dh=dh, ds=ds), q3 + k)
    total = hidden[...] + down[yh, mine]
    for k in range(7):
        arrived(down_in.at[k], q3 + k)
        total = total + down_in[k].astype(F32)
    fin[0] = total[:, :128]
    fin[1] = total[:, 128:]

    for r in range(3):
        for j in range(2):
            send1[pl.ds(2 * r + j, 32, stride=8), :] = fin[j, pl.ds(r, 32, stride=3), :]
    for j in range(2):
        send1[pl.ds(6 + j, 32, stride=8), :] = jnp.zeros((32, 128), F32)
    blocks = send1.reshape(4, 8, 8, 128)
    f1 = ids(7)
    for d in range(1, 8):
        send(blocks.at[:, zs[d]], mid.at[z], dev(dz=d), f1 + d - 1)
    mid[z] = blocks[:, z]
    for d in range(1, 8):
        arrived(mid.at[lax.rem(z + 8 - d, 8)], f1 + d - 1)

    f2 = ids(16)
    for xl in range(2):
        for ny in range(2):
            for nh in range(2):
                nx = 2 * h + xl
                own = (nx == x) & (ny == yh) & (nh == h)

                @pl.when(own)
                def _():
                    out[xy] = mid[:, 2 * xl + ny]

                send(
                    mid.at[:, 2 * xl + ny], out.at[xy], ((nx * 2 + ny) * 8 + z, nh, s),
                    f2 + 4 * xl + 2 * ny + nh, jnp.logical_not(own), slot=f2 + xy,
                )
    for k in range(8):
        own = (xy == k) & (h == x // 2)

        @pl.when(jnp.logical_not(own))
        def _():
            arrived(out.at[k], f2 + k)

    for ref, index, condition in pending:
        when(condition, lambda: copy_of(ref, ref, dev(dh=1), index, index).wait_send())
    assert counter[0] <= SEMS


SEMS = 320


def layer(
    lengths, queries, new_keys, new_values, key_cache, value_cache,
    residual, gain, out_weight, gate_weight, up_weight, down_weight,
):
    vmem = pl.BlockSpec(memory_space=pltpu.VMEM)
    anywhere = pl.BlockSpec(memory_space=pl.ANY)
    scratch = [
        pltpu.VMEM((3, 2048, 256), BF),
        pltpu.VMEM((3, 2048, 256), BF),
        pltpu.VMEM((3, 2, 16, HS), BF),
        pltpu.VMEM((2048, 256), BF),
        pltpu.VMEM((2, 256, UNITS), BF),
        pltpu.VMEM((2, 256, UNITS), BF),
        pltpu.VMEM((2, UNITS, 256), BF),
        pltpu.VMEM((2, 64, 3, 16, HS), BF),
        pltpu.VMEM((64 * 3 * 16, HS), F32),
        pltpu.VMEM((4, 96, 256), F32),
        pltpu.VMEM((4, 96, 256), BF),
        pltpu.VMEM((3, 96, 256), BF),
        pltpu.VMEM((96, 256), F32),
        pltpu.VMEM((2, 4, 96, 256), BF),
        pltpu.VMEM((2, 4, 8, 128), F32),
        pltpu.VMEM((2, 8, 128), F32),
        pltpu.VMEM((10, 8, 128), F32),
        pltpu.VMEM((8, 128), F32),
        pltpu.VMEM((2, 4, 2, NA, 48, 128), BF),
        pltpu.VMEM((2, 2, NA, 48, 128), BF),
        pltpu.VMEM((2, 2, 2, NA, 48, 128), BF),
        pltpu.VMEM((2, 2, NA, 48, 128), BF),
        pltpu.VMEM((2, 7, 2, 48, 128), BF),
        pltpu.VMEM((2, 8, FLAT, 128), BF),
        pltpu.VMEM((2, 2, 4, FLAT, 128), BF),
        pltpu.VMEM((2, FLAT, 128), BF),
        pltpu.VMEM((2, 3, FLAT // 4, 128), BF),
        pltpu.VMEM((3, 16, 128), F32),
        pltpu.VMEM((4, NA, 96, 128), BF),
        pltpu.VMEM((8, FLAT, 128), BF),
        pltpu.VMEM((2, 4, 96, 256), F32),
        pltpu.VMEM((2, 4, 96, 256), BF),
        pltpu.VMEM((7, 96, 256), BF),
        pltpu.VMEM((2, 96, 128), F32),
        pltpu.VMEM((256, 128), F32),
        pltpu.VMEM((8, 4, 8, 128), F32),
        pltpu.SemaphoreType.DMA((6,)),
        pltpu.SemaphoreType.DMA((4,)),
        pltpu.SemaphoreType.DMA((SEMS,)),
        pltpu.SemaphoreType.DMA((SEMS,)),
    ]
    return pl.pallas_call(
        layer_kernel,
        out_shape=jax.ShapeDtypeStruct((8, 8, 8, 128), F32),
        in_specs=[pl.BlockSpec(memory_space=pltpu.SMEM), vmem, vmem, vmem, anywhere, anywhere, vmem, vmem] + [anywhere] * 4,
        out_specs=vmem,
        scratch_shapes=scratch,
        compiler_params=pltpu.CompilerParams(collective_id=0, has_side_effects=True, vmem_limit_bytes=VMEM_LIMIT),
        cost_estimate=pl.CostEstimate(flops=2 * 384 * 256 * 12032, bytes_accessed=8 * 2**20, transcendentals=0),
        name="layer",
    )(lengths, queries, new_keys, new_values, key_cache, value_cache, residual.reshape(4, 96, 256), gain, out_weight, gate_weight, up_weight, down_weight)


def body(
    queries,
    new_keys,
    new_values,
    key_cache,
    value_cache,
    cache_lengths,
    residual,
    norm_gain,
    out_weight,
    gate_weight,
    up_weight,
    down_weight,
):
    rows = layer(
        cache_lengths, queries[0], new_keys[0], new_values[0], key_cache[0], value_cache[0],
        residual, norm_gain, out_weight, gate_weight, up_weight, down_weight,
    )
    rows = rows.reshape(64, 8, HS)[:, :6].reshape(64, 3, 2 * HS)
    return rows.transpose(1, 0, 2).reshape(1, 3, D).astype(BF)


def solution(mesh):
    return jax.shard_map(
        body,
        mesh=mesh,
        in_specs=(
            P("side", "dp", "head"),
            P("side", "dp", "head"),
            P("side", "dp", "head"),
            P("side", "dp", None, "head"),
            P("side", "dp", None, "head"),
            P("side", "dp"),
            P(None, None, "dp"),
            P("dp"),
            P(("head", "side"), "dp"),
            P("dp", ("head", "side")),
            P("dp", ("head", "side")),
            P(("head", "side"), "dp"),
        ),
        out_specs=P("side", "dp", None),
        check_vma=False,
    )
```

```python
import math

import jax
import jax.numpy as jnp
from jax import lax
from jax.experimental import pallas as pl
from jax.experimental.pallas import tpu as pltpu
from jax.sharding import PartitionSpec as P

D = 16384
HS = 128
BF = jnp.bfloat16
F32 = jnp.float32
MESH = pl.DeviceIdType.MESH
VMEM_LIMIT = 56 * 2**20

UNITS = 1664
NA = 8
NB = 5
PUSH = (1, 4, 1)
FLAT = 256


def attend_row(length, q, new_key, new_value, keys, values):
    span = keys.shape[0]
    zero = jnp.zeros((16, HS), F32)
    wide = jnp.concatenate(
        [jnp.concatenate([q[:16], zero], axis=1), jnp.concatenate([zero, q[16:]], axis=1)], axis=0
    )
    scale = 1.0 / math.sqrt(HS)
    nt = (((1,), (1,)), ((), ()))
    scores = lax.dot_general(wide.astype(BF), keys, nt, preferred_element_type=F32) * scale
    fresh = jnp.sum(wide * new_key, axis=1, keepdims=True) * scale
    valid = lax.broadcasted_iota(jnp.int32, (32, span), 1) < length
    masked = jnp.where(valid, scores, -jnp.inf)
    highest = jnp.maximum(jnp.max(masked, axis=1, keepdims=True), fresh)
    probs = jnp.exp(masked - highest)
    fresh_prob = jnp.exp(fresh - highest)
    total = jnp.sum(probs, axis=1, keepdims=True) + fresh_prob
    inverse = 1.0 / total
    weights = (probs * inverse).astype(BF)
    fresh_weight = (fresh_prob * inverse).astype(BF).astype(F32)
    mixed = jnp.dot(weights, values, preferred_element_type=F32) + fresh_weight * new_value
    return mixed[:16, :HS].astype(BF), mixed[16:, HS:].astype(BF)


def layer_kernel(
    lengths, queries, new_keys, new_values, key_hbm, value_hbm,
    res, gain, wo_hbm, wg_hbm, wu_hbm, wd_hbm,
    out,
    keys, values, att, wo, wg, wu, wd,
    seen, wide, part, part_bf, quarter_in, hidden, scaled,
    squares_mine, squares, squares_in, squares_all,
    pa, pa_in1, pa_in2, za, za_in,
    pb, pb_in, xb, xb_in, scale_rows,
    act_a, act_b, down, down_bf, down_in, fin, send1, send1_bf, mid, mid_wide, send2, final, final_wide,
    csem, wsem, ss, rs,
):
    dp = lax.axis_index("dp")
    h = lax.axis_index("head")
    s = lax.axis_index("side")
    z = lax.rem(dp, 8)
    xy = dp // 8
    yh = lax.rem(xy, 2)
    x = xy // 2
    mine = 2 * s + h

    def dev(dx=0, dy=0, dz=0, dh=0, ds=0):
        nx = lax.rem(x + (dx + 4), 4)
        ny = lax.rem(yh + dy, 2)
        nz = lax.rem(z + (dz + 8), 8)
        return ((nx * 2 + ny) * 8 + nz, lax.rem(h + dh, 2), lax.rem(s + ds, 2))

    counter = [0]
    pending = []

    def ids(count):
        first = counter[0]
        counter[0] += count
        return first

    def when(condition, action):
        if condition is None:
            action()
        else:
            pl.when(condition)(action)

    def copy_of(src, dst, target, send_index, recv_index):
        return pltpu.make_async_remote_copy(
            src_ref=src, dst_ref=dst, send_sem=ss.at[send_index], recv_sem=rs.at[recv_index],
            device_id=target, device_id_type=MESH,
        )

    def send(src, dst, target, index, condition=None, slot=None):
        when(condition, copy_of(src, dst, target, index, index if slot is None else slot).start)
        pending.append((src, index, condition))

    def arrived(ref, index):
        copy_of(ref, ref, dev(dh=1), index, index).wait_recv()

    caches = []
    for r in range(3):
        for k, (src, dst) in enumerate(((key_hbm, keys), (value_hbm, values))):
            copy = pltpu.make_async_copy(src.at[r], dst.at[r], csem.at[2 * r + k])
            copy.start()
            caches.append(copy)

    plane = [(dx, dy) for dx in range(4) for dy in range(2)]
    peers = [dict(dx=dx, dy=dy, dh=dh) for dx, dy in plane for dh in range(2) if dx or dy or dh]
    peers += [dict(dz=dz) for dz in range(1, 8)]
    peers += [dict(dy=dy, dh=dh, ds=1) for dy in range(2) for dh in range(2)]
    barrier = pltpu.get_barrier_semaphore()
    for peer in peers:
        pl.semaphore_signal(barrier, inc=1, device_id=dev(**peer), device_id_type=MESH)

    loads = []

    def load(src, dst):
        copy = pltpu.make_async_copy(src, dst, wsem.at[len(loads)])
        copy.start()
        loads.append(copy)

    units = pl.ds(pl.multiple_of(UNITS * yh, 128), UNITS)
    others = pl.ds(pl.multiple_of(UNITS * (1 - yh), 128), UNITS)
    w_id = ids(7)
    cuts = [(u, 128 * NA, 128 * NB) for u in range(2)]
    cuts += [(u, 64 * NA * k, 64 * NA) for u in range(2) for k in range(2)]
    pieces = [
        (
            (wg_hbm, wu_hbm)[u].at[:, pl.ds(pl.multiple_of(UNITS * (1 - yh) + first, 128), count)],
            (wg, wu)[u].at[yh, :, pl.ds(first, count)],
        )
        for u, first, count in cuts
    ]
    pushed = [0]

    def push(count):
        for _ in range(count):
            src, dst = pieces[pushed[0]]
            send(src, dst, dev(dy=1), w_id + pushed[0])
            pushed[0] += 1

    for r in range(3):
        q = queries[...].astype(F32)[r : r + 1]
        q = jnp.concatenate([q[:, HS * g : HS * g + HS] for g in range(32)], axis=0)
        caches[2 * r].wait()
        caches[2 * r + 1].wait()
        if r == 0:
            pl.semaphore_wait(barrier, len(peers))
            push(PUSH[0])
        if r == 2:
            load(wo_hbm, wo)
            load(wg_hbm.at[:, units], wg.at[yh])
            load(wu_hbm.at[:, units], wu.at[yh])
            load(wd_hbm.at[units], wd.at[yh])
        low, high = attend_row(
            lengths[0, r], q, new_keys[...].astype(F32)[r : r + 1], new_values[...].astype(F32)[r : r + 1],
            keys[r], values[r],
        )
        att[r, 0] = low
        att[r, 1] = high

    y_id = ids(4)
    for ny in range(2):
        for ns in range(2):
            if ny or ns:
                head = s if ns == 0 else 1 - s
                send(att.at[:, head], seen.at[s, dp], dev(dy=ny, ds=ns), y_id + 2 * ny + ns)
    seen[s, dp] = att[:, s]

    za_id = ids(8)
    xa_id = ids(8 * 3)
    xyb_id = ids(8)
    zb_id = ids(16)

    def slot(nx, ny, nz):
        return (nx * 2 + ny) * 8 + nz

    xs = [lax.rem(x + d, 4) for d in range(4)]
    zs = [lax.rem(z + d, 8) for d in range(8)]
    ys = [yh, 1 - yh]

    arrived(seen.at[1 - s, dp], y_id + 1)
    there = slot(x, ys[1], z)
    arrived(seen.at[s, there], y_id + 2)
    arrived(seen.at[1 - s, there], y_id + 3)

    push(PUSH[1])

    seen8 = seen.at[0].reshape(4, 2, 8, 3, 16, HS)

    def pair_ref(nx, nz):
        return seen8.at[nx, :, nz]

    for d in range(1, 8):
        send(pair_ref(x, z), pair_ref(x, z), dev(dz=d), za_id + d)
    for j in range(1, 4):
        send(pair_ref(x, z), pair_ref(x, z), dev(dx=j), xa_id + j - 1)

    seenx = seen.at[1].reshape(4, 2, 8, 3, 16, HS)
    for j in range(1, 4):
        send(seenx.at[x, :, z], seenx.at[x, :, z], dev(dx=j), xyb_id + j)
    for j in range(1, 4):
        arrived(seenx.at[lax.rem(x + 4 - j, 4), :, z], xyb_id + j)
    seenz = seen.at[1].reshape(8, 8, 3, 16, HS)

    def ring(step, towards, which):
        return seenz.at[pl.ds(4 * which, 4), lax.rem(z + 8 - towards * (step - 1), 8)]

    def ring_id(step, towards, which):
        return zb_id + step * 4 + 2 * which + (0 if towards > 0 else 1)

    def last(towards):
        return 0 if towards > 0 else 1

    for which in range(2):
        for t in (1, -1):
            send(ring(1, t, which), ring(1, t, which), dev(dz=t), ring_id(0, t, which))

    plan = {1: (1, 7), 2: (2, 6), 3: (3, 5), 4: (4,)}
    for step in range(1, 5):
        for d in plan[step]:
            nz = zs[8 - d]
            arrived(pair_ref(x, nz), za_id + d)
            for j in range(1, 4):
                send(pair_ref(x, nz), pair_ref(x, nz), dev(dx=j), xa_id + 3 * d + j - 1)
        for which in range(2):
            for t in (1, -1):
                if step == 4 and which != last(t):
                    continue
                arrived(ring(step + 1, t, which), ring_id(step - 1, t, which))
                if step < 3 or (step == 3 and which == last(t)):
                    send(ring(step + 1, t, which), ring(step + 1, t, which), dev(dz=t), ring_id(step, t, which))

    loads[0].wait()

    def project(m):
        wide[...] = seen[m].reshape(64 * 3 * 16, HS).astype(F32)
        total = jnp.zeros((192, 256), F32)
        for g in range(8):
            left_half = wide[pl.ds(2 * g, 192, stride=16), :]
            right_half = wide[pl.ds(2 * g + 1, 192, stride=16), :]
            piece = jnp.concatenate([left_half, right_half], axis=1).astype(BF)
            total = total + jnp.dot(piece, wo[256 * g : 256 * g + 256, :], preferred_element_type=F32)
        for k in range(2):
            part[2 * m + k] = total[96 * k : 96 * k + 96]
            part_bf[2 * m + k] = total[96 * k : 96 * k + 96].astype(BF)

    project(1)
    for d in range(8):
        nz = lax.rem(z + 8 - d, 8)
        for j in range(1, 4):
            arrived(pair_ref(lax.rem(x + 4 - j, 4), nz), xa_id + 3 * d + j - 1)
    project(0)

    group = [(1, 0), (0, 1), (1, 1)]
    q1 = ids(3)
    for k, (dh, ds) in enumerate(group):
        there = 2 * lax.rem(s + ds, 2) + lax.rem(h + dh, 2)
        send(part_bf.at[there], quarter_in.at[k], dev(dh=dh, ds=ds), q1 + k)
    total = res[mine].astype(F32) + part[mine]
    for k in range(3):
        arrived(quarter_in.at[k], q1 + k)
        total = total + quarter_in[k].astype(F32)
    hidden[...] = total
    scaled[yh, mine] = (total * gain[...].reshape(1, 256).astype(F32)).astype(BF)
    group8 = [(dy, dh, ds) for dy in range(2) for dh in range(2) for ds in range(2)][1:]
    q2 = ids(7)

    def quarter(dh, ds):
        return 2 * lax.rem(s + ds, 2) + lax.rem(h + dh, 2)

    for k, (dy, dh, ds) in enumerate(group8):
        send(scaled.at[yh, mine], scaled.at[yh, mine], dev(dy=dy, dh=dh, ds=ds), q2 + k)

    row_square = jnp.sum(total * total, axis=1, keepdims=True)
    diagonal = lax.broadcasted_iota(jnp.int32, (96, 128), 0) == lax.broadcasted_iota(jnp.int32, (96, 128), 1)
    lanes = jnp.sum(jnp.where(diagonal, row_square, 0.0), axis=0, keepdims=True)
    squares_mine[yh, mine] = jnp.broadcast_to(lanes, (8, 128))
    sg, sx, sz = ids(7), ids(3), ids(7)
    for k, (dy, dh, ds) in enumerate(group8):
        send(squares_mine.at[yh, mine], squares_mine.at[yh, mine], dev(dy=dy, dh=dh, ds=ds), sg + k)

    def squares_x():
        for k, (dy, dh, ds) in enumerate(group8):
            arrived(squares_mine.at[ys[dy], quarter(dh, ds)], sg + k)
        row = lax.broadcasted_iota(jnp.int32, (8, 128), 0)
        value = jnp.zeros((8, 128), F32)
        for k in range(4):
            value = value + jnp.where(row == k, squares_mine[0, k] + squares_mine[1, k], 0.0)
        squares[0] = value
        for j in range(1, 4):
            send(squares.at[0], squares_in.at[j - 1], dev(dx=j), sx + j - 1)

    def squares_z():
        for j in range(3):
            arrived(squares_in.at[j], sx + j)
        squares[1] = squares[0] + squares_in[0] + squares_in[1] + squares_in[2]
        for d in range(1, 8):
            send(squares.at[1], squares_in.at[2 + d], dev(dz=d), sz + d - 1)

    def squares_done():
        value = squares[1]
        for d in range(1, 8):
            arrived(squares_in.at[2 + d], sz + d - 1)
            value = value + squares_in[2 + d]
        squares_all[...] = lax.rsqrt(value / D + 1e-05)

    for k, (dy, dh, ds) in enumerate(group8):
        arrived(scaled.at[ys[dy], quarter(dh, ds)], q2 + k)

    rows = jnp.concatenate([scaled[0].reshape(384, 256), scaled[1].reshape(384, 256)], axis=1)
    xa1, xa2, xa3 = ids(4), ids(4), ids(4)
    zb = ids(16)
    zra = ids(14)
    xyr = ids(6)
    weight = (wg, wu)
    back = [lax.rem(x + 4 - d, 4) for d in range(4)]
    def multiply(u, c, count):
        columns = weight[u][:, :, 128 * c : 128 * (c + count)].reshape(512, 128 * count)
        value = jnp.dot(rows, columns, preferred_element_type=F32).astype(BF)
        return [value[:, 128 * i : 128 * i + 128] for i in range(count)]

    def multiply_a(u):
        for c in range(0, NA, 2):
            for i, value in enumerate(multiply(u, c, 2)):
                pa[u, :, :, c + i] = value.reshape(4, 2, 48, 128)
        send(pa.at[u, xs[2], 0], pa_in1.at[u, 0], dev(dx=1), xa1 + 2 * u)
        send(pa.at[u, xs[2], 1], pa_in1.at[u, 1], dev(dx=-1), xa1 + 2 * u + 1)
        send(pa.at[u, xs[1], 1], pa_in2.at[u, 0, 1], dev(dx=1), xa2 + 2 * u)
        send(pa.at[u, xs[3], 0], pa_in2.at[u, 1, 0], dev(dx=-1), xa2 + 2 * u + 1)

    def half(towards):
        return pl.ds(0 if towards > 0 else FLAT // 2, FLAT // 2)

    def z_block(u, dist, towards):
        there = lax.rem(z + 8 + towards * dist, 8)
        if dist == 4:
            return pb.at[u, there, half(towards)]
        return pb.at[u, there]

    def z_in(u, dist, towards):
        dst = pb_in.at[u, 0 if towards > 0 else 1, dist - 1]
        if dist == 4:
            return dst.at[half(towards)]
        return dst

    def z_id(u, dist, towards):
        return zb + 8 * u + 2 * (dist - 1) + (0 if towards > 0 else 1)

    def z_send(u, dist):
        for t in (1, -1):
            send(z_block(u, dist, t), z_in(u, dist, t), dev(dz=t), z_id(u, dist, t))

    def multiply_b(u):
        for c in range(0, NB, 2):
            for i, value in enumerate(multiply(u, NA + c, min(2, NB - c))):
                pb[u, :, 48 * (c + i) : 48 * (c + i) + 48] = value.reshape(8, 48, 128)
        pb[u, :, 48 * NB :] = jnp.zeros((8, FLAT - 48 * NB, 128), BF)
        z_send(u, 4)

    def z_step(u, dist):
        for t in (1, -1):
            arrived(z_in(u, dist, t), z_id(u, dist, t))
            there = lax.rem(z + 8 + t * (dist - 1), 8)
            d = 0 if t > 0 else 1
            part_rows = half(t) if dist == 4 else pl.ds(0, FLAT)
            pb[u, there, part_rows] = (
                pb[u, there, part_rows].astype(F32) + pb_in[u, d, dist - 1, part_rows].astype(F32)
            ).astype(BF)
        z_send(u, dist - 1)

    def x_step(u):
        arrived(pa_in1.at[u, 0], xa1 + 2 * u)
        pa[u, xs[1], 0] = (pa[u, xs[1], 0].astype(F32) + pa_in1[u, 0].astype(F32)).astype(BF)
        send(pa.at[u, xs[1], 0], pa_in2.at[u, 0, 0], dev(dx=1), xa3 + 2 * u)
        arrived(pa_in1.at[u, 1], xa1 + 2 * u + 1)
        pa[u, xs[3], 1] = (pa[u, xs[3], 1].astype(F32) + pa_in1[u, 1].astype(F32)).astype(BF)
        send(pa.at[u, xs[3], 1], pa_in2.at[u, 1, 1], dev(dx=-1), xa3 + 2 * u + 1)

    def x_done(u):
        arrived(pa_in2.at[u, 0, 1], xa2 + 2 * u)
        arrived(pa_in2.at[u, 1, 0], xa2 + 2 * u + 1)
        arrived(pa_in2.at[u, 0, 0], xa3 + 2 * u)
        arrived(pa_in2.at[u, 1, 1], xa3 + 2 * u + 1)
        for k in range(2):
            za[u, k] = (
                pa[u, x, k].astype(F32) + pa_in2[u, 0, k].astype(F32) + pa_in2[u, 1, k].astype(F32)
            ).astype(BF)
        for d in range(1, 8):
            send(za.at[u, :, zs[d]], za_in.at[u, d - 1], dev(dz=d), zra + 7 * u + d - 1)

    def own_flat(nx):
        return pl.ds(pl.multiple_of(FLAT // 4 * nx, FLAT // 4), FLAT // 4)

    def xb_start(u):
        for t in (1, -1):
            arrived(z_in(u, 1, t), z_id(u, 1, t))
        xb[u] = (
            pb[u, z].astype(F32) + pb_in[u, 0, 0].astype(F32) + pb_in[u, 1, 0].astype(F32)
        ).astype(BF)
        for j in range(1, 4):
            send(xb.at[u, own_flat(xs[j])], xb_in.at[u, j - 1], dev(dx=j), xyr + 3 * u + j - 1)

    squares_x()
    push(PUSH[2])
    loads[1].wait()
    loads[2].wait()
    def weights_there(*numbers):
        for k in numbers:
            u, first, count = cuts[k]
            arrived(weight[u].at[1 - yh, :, pl.ds(first, count)], w_id + k)

    for u in range(2):
        weights_there(u)
        multiply_b(u)
    weights_there(2, 3)
    multiply_a(0)
    z_step(0, 4)
    z_step(1, 4)
    weights_there(4, 5)
    send(wd_hbm.at[others], wd.at[yh], dev(dy=1), w_id + 6)
    multiply_a(1)
    x_step(0)
    z_step(0, 3)
    z_step(1, 3)
    squares_z()
    x_step(1)
    x_done(0)
    z_step(0, 2)
    z_step(1, 2)
    x_done(1)
    squares_done()
    xb_start(0)
    xb_start(1)

    def scaling(index, offset, count):
        lane_scale = squares_all[pl.ds(index, 1)]
        pick = (
            lax.broadcasted_iota(jnp.int32, (count, 128), 0) + offset
            == lax.broadcasted_iota(jnp.int32, (count, 128), 1)
        )
        return jnp.sum(jnp.where(pick, lane_scale, 0.0), axis=1, keepdims=True)

    def activate(gate, upper, scale):
        gate = gate * scale
        return (gate / (1.0 + jnp.exp(-gate)) * (upper * scale)).astype(BF)

    ga, gax = ids(8), ids(24)
    gb, gbz = ids(4), ids(8)

    scale_rows[...] = jnp.broadcast_to(scaling(z // 2, 48 * lax.rem(z, 2), 48), (48, 128)).reshape(3, 16, 128)
    sums = []
    for u in range(2):
        value = xb[u, own_flat(x)].astype(F32)
        for j in range(3):
            arrived(xb_in.at[u, j], xyr + 3 * u + j)
            value = value + xb_in[u, j].astype(F32)
        sums.append(value)
    tiles = [scale_rows[lax.rem(4 * x + i, 3)] for i in range(4)]
    act_b[z, own_flat(x)] = activate(sums[0], sums[1], jnp.concatenate(tiles, axis=0))
    for j in range(1, 4):
        send(act_b.at[z, own_flat(x)], act_b.at[z, own_flat(x)], dev(dx=j), gb + j)

    sums = []
    for u in range(2):
        value = za[u, :, z].astype(F32)
        for d in range(1, 8):
            arrived(za_in.at[u, d - 1], zra + 7 * u + d - 1)
            value = value + za_in[u, d - 1].astype(F32)
        sums.append(value.reshape(96, 128))
    act_a[x, z] = activate(sums[0], sums[1], scaling(x, 0, 96))
    for d in range(1, 8):
        send(act_a.at[x, z], act_a.at[x, z], dev(dz=d), ga + d)
    for j in range(1, 4):
        send(act_a.at[x, z], act_a.at[x, z], dev(dx=j), gax + j - 1)

    for j in range(1, 4):
        arrived(act_b.at[z, own_flat(back[j])], gb + j)

    def gz_id(dist, towards):
        return gbz + 2 * (dist - 1) + (0 if towards > 0 else 1)

    for t in (1, -1):
        for dist in (2, 1):
            send(act_b.at[z], act_b.at[z], dev(dz=t * dist), gz_id(dist, t))

    def a_step(d):
        nz = zs[(8 - d) % 8]
        arrived(act_a.at[x, nz], ga + d)
        for j in range(1, 4):
            send(act_a.at[x, nz], act_a.at[x, nz], dev(dx=j), gax + 3 * d + j - 1)

    a_step(1)
    a_step(7)
    for t in (1, -1):
        far = act_b.at[zs[(8 - 2 * t) % 8]]
        arrived(far, gz_id(2, t))
        send(far, far, dev(dz=t), gz_id(3, t))
        send(far.at[half(t)], far.at[half(t)], dev(dz=2 * t), gz_id(4, t))
    for d in (2, 6, 3, 5, 4):
        a_step(d)
    for t in (1, -1):
        arrived(act_b.at[zs[(8 - t) % 8]], gz_id(1, t))
        arrived(act_b.at[zs[(8 - 3 * t) % 8]], gz_id(3, t))
        arrived(act_b.at[zs[4], half(t)], gz_id(4, t))

    loads[3].wait()
    arrived(wd.at[1 - yh], w_id + 6)

    def lower(chunks, first):
        for i in range(0, len(chunks), 2):
            pieces, numbers = zip(*chunks[i : i + 2])
            piece = jnp.concatenate(pieces, axis=1) if len(pieces) == 2 else pieces[0]
            depth = pl.ds(128 * numbers[0], 128 * len(numbers))
            for ny in range(2):
                value = jnp.dot(piece, wd[ny, depth], preferred_element_type=F32).reshape(4, 96, 256)
                if first and i == 0:
                    down[ny] = value
                else:
                    down[ny] += value

    lower([(act_b[:, 48 * c : 48 * c + 48].reshape(384, 128), NA + c) for c in range(NB)], True)
    for d in range(8):
        for j in range(1, 4):
            arrived(act_a.at[back[j], zs[(8 - d) % 8]], gax + 3 * d + j - 1)
    lower([(act_a[:, c].reshape(384, 128), c) for c in range(NA)], False)
    down_bf[...] = down[...].astype(BF)

    q3 = ids(7)
    for k, (dy, dh, ds) in enumerate(group8):
        send(down_bf.at[ys[dy], quarter(dh, ds)], down_in.at[k], dev(dy=dy, dh=dh, ds=ds), q3 + k)
    total = hidden[...] + down[yh, mine]
    for k in range(7):
        arrived(down_in.at[k], q3 + k)
        total = total + down_in[k].astype(F32)
    fin[0] = total[:, :128]
    fin[1] = total[:, 128:]

    for r in range(3):
        for j in range(2):
            value = fin[j, pl.ds(r, 32, stride=3), :]
            for k in range(4):
                send1[pl.ds((2 * r + j) * 4 + k, 8, stride=32), :] = value[8 * k : 8 * k + 8]
    for k in range(8):
        send1[pl.ds(24 + k, 8, stride=32), :] = jnp.zeros((8, 128), F32)
    send1_bf[...] = send1[...].astype(BF).reshape(8, 32, 128)
    f1 = ids(7)
    for d in range(1, 8):
        send(send1_bf.at[zs[d]], mid.at[z], dev(dz=d), f1 + d - 1)
    mid[z] = send1_bf[z]
    for d in range(1, 8):
        arrived(mid.at[zs[8 - d]], f1 + d - 1)
    mid_wide[...] = mid[...].astype(F32).reshape(256, 128)
    for k in range(4):
        rows_k = [mid_wide[pl.ds(4 * i + k, 8, stride=32), :] for i in range(6)]
        send2[k] = jnp.concatenate(rows_k, axis=0).astype(BF)

    f2 = ids(16)
    for xl in range(2):
        for ny in range(2):
            for nh in range(2):
                nx = 2 * h + xl
                own = (nx == x) & (ny == yh) & (nh == h)

                @pl.when(own)
                def _():
                    final[xy] = send2[2 * xl + ny]

                send(
                    send2.at[2 * xl + ny], final.at[xy], ((nx * 2 + ny) * 8 + z, nh, s),
                    f2 + 4 * xl + 2 * ny + nh, jnp.logical_not(own), slot=f2 + xy,
                )
    for k in range(8):
        own = (xy == k) & (h == x // 2)

        @pl.when(jnp.logical_not(own))
        def _():
            arrived(final.at[k], f2 + k)

    final_wide[...] = final[...].astype(F32).reshape(384, 128)
    for k in range(8):
        columns = [final_wide[pl.ds(48 * k + 8 * j + i, 3, stride=16), :] for i in range(8) for j in range(2)]
        out[:, 2048 * k : 2048 * k + 2048] = jnp.concatenate(columns, axis=1).astype(BF)

    for ref, index, condition in pending:
        when(condition, lambda: copy_of(ref, ref, dev(dh=1), index, index).wait_send())
    assert counter[0] <= SEMS


SEMS = 320


def layer(
    lengths, queries, new_keys, new_values, key_cache, value_cache,
    residual, gain, out_weight, gate_weight, up_weight, down_weight,
):
    vmem = pl.BlockSpec(memory_space=pltpu.VMEM)
    anywhere = pl.BlockSpec(memory_space=pl.ANY)
    scratch = [
        pltpu.VMEM((3, 2048, 256), BF),
        pltpu.VMEM((3, 2048, 256), BF),
        pltpu.VMEM((3, 2, 16, HS), BF),
        pltpu.VMEM((2048, 256), BF),
        pltpu.VMEM((2, 256, UNITS), BF),
        pltpu.VMEM((2, 256, UNITS), BF),
        pltpu.VMEM((2, UNITS, 256), BF),
        pltpu.VMEM((2, 64, 3, 16, HS), BF),
        pltpu.VMEM((64 * 3 * 16, HS), F32),
        pltpu.VMEM((4, 96, 256), F32),
        pltpu.VMEM((4, 96, 256), BF),
        pltpu.VMEM((3, 96, 256), BF),
        pltpu.VMEM((96, 256), F32),
        pltpu.VMEM((2, 4, 96, 256), BF),
        pltpu.VMEM((2, 4, 8, 128), F32),
        pltpu.VMEM((2, 8, 128), F32),
        pltpu.VMEM((10, 8, 128), F32),
        pltpu.VMEM((8, 128), F32),
        pltpu.VMEM((2, 4, 2, NA, 48, 128), BF),
        pltpu.VMEM((2, 2, NA, 48, 128), BF),
        pltpu.VMEM((2, 2, 2, NA, 48, 128), BF),
        pltpu.VMEM((2, 2, NA, 48, 128), BF),
        pltpu.VMEM((2, 7, 2, 48, 128), BF),
        pltpu.VMEM((2, 8, FLAT, 128), BF),
        pltpu.VMEM((2, 2, 4, FLAT, 128), BF),
        pltpu.VMEM((2, FLAT, 128), BF),
        pltpu.VMEM((2, 3, FLAT // 4, 128), BF),
        pltpu.VMEM((3, 16, 128), F32),
        pltpu.VMEM((4, NA, 96, 128), BF),
        pltpu.VMEM((8, FLAT, 128), BF),
        pltpu.VMEM((2, 4, 96, 256), F32),
        pltpu.VMEM((2, 4, 96, 256), BF),
        pltpu.VMEM((7, 96, 256), BF),
        pltpu.VMEM((2, 96, 128), F32),
        pltpu.VMEM((256, 128), F32),
        pltpu.VMEM((8, 32, 128), BF),
        pltpu.VMEM((8, 32, 128), BF),
        pltpu.VMEM((256, 128), F32),
        pltpu.VMEM((4, 48, 128), BF),
        pltpu.VMEM((8, 48, 128), BF),
        pltpu.VMEM((384, 128), F32),
        pltpu.SemaphoreType.DMA((6,)),
        pltpu.SemaphoreType.DMA((4,)),
        pltpu.SemaphoreType.DMA((SEMS,)),
        pltpu.SemaphoreType.DMA((SEMS,)),
    ]
    return pl.pallas_call(
        layer_kernel,
        out_shape=jax.ShapeDtypeStruct((3, D), BF),
        in_specs=[pl.BlockSpec(memory_space=pltpu.SMEM), vmem, vmem, vmem, anywhere, anywhere, vmem, vmem] + [anywhere] * 4,
        out_specs=vmem,
        scratch_shapes=scratch,
        compiler_params=pltpu.CompilerParams(collective_id=0, has_side_effects=True, vmem_limit_bytes=VMEM_LIMIT),
        cost_estimate=pl.CostEstimate(flops=2 * 384 * 256 * 12032, bytes_accessed=8 * 2**20, transcendentals=0),
        name="layer",
    )(lengths, queries, new_keys, new_values, key_cache, value_cache, residual.reshape(4, 96, 256), gain, out_weight, gate_weight, up_weight, down_weight)


def body(
    queries,
    new_keys,
    new_values,
    key_cache,
    value_cache,
    cache_lengths,
    residual,
    norm_gain,
    out_weight,
    gate_weight,
    up_weight,
    down_weight,
):
    rows = layer(
        cache_lengths, queries[0], new_keys[0], new_values[0], key_cache[0], value_cache[0],
        residual, norm_gain, out_weight, gate_weight, up_weight, down_weight,
    )
    return rows.reshape(1, 3, D)


def solution(mesh):
    return jax.shard_map(
        body,
        mesh=mesh,
        in_specs=(
            P("side", "dp", "head"),
            P("side", "dp", "head"),
            P("side", "dp", "head"),
            P("side", "dp", None, "head"),
            P("side", "dp", None, "head"),
            P("side", "dp"),
            P(None, None, "dp"),
            P("dp"),
            P(("head", "side"), "dp"),
            P("dp", ("head", "side")),
            P("dp", ("head", "side")),
            P(("head", "side"), "dp"),
        ),
        out_specs=P("side", "dp", None),
        check_vma=False,
    )
```

```python
import math

import jax
import jax.numpy as jnp
from jax import lax
from jax.experimental import pallas as pl
from jax.experimental.pallas import tpu as pltpu
from jax.sharding import PartitionSpec as P

D = 16384
HS = 128
BF = jnp.bfloat16
F32 = jnp.float32
MESH = pl.DeviceIdType.MESH
VMEM_LIMIT = 56 * 2**20

UNITS = 1664
NA = 8
NB = 5
PUSH = (1, 4, 1)
FLAT = 256


def attend_row(length, q, new_key, new_value, keys, values):
    span = keys.shape[0]
    zero = jnp.zeros((16, HS), F32)
    wide = jnp.concatenate(
        [jnp.concatenate([q[:16], zero], axis=1), jnp.concatenate([zero, q[16:]], axis=1)], axis=0
    )
    scale = 1.0 / math.sqrt(HS)
    nt = (((1,), (1,)), ((), ()))
    scores = lax.dot_general(wide.astype(BF), keys, nt, preferred_element_type=F32) * scale
    fresh = jnp.sum(wide * new_key, axis=1, keepdims=True) * scale
    valid = lax.broadcasted_iota(jnp.int32, (32, span), 1) < length
    masked = jnp.where(valid, scores, -jnp.inf)
    highest = jnp.maximum(jnp.max(masked, axis=1, keepdims=True), fresh)
    probs = jnp.exp(masked - highest)
    fresh_prob = jnp.exp(fresh - highest)
    total = jnp.sum(probs, axis=1, keepdims=True) + fresh_prob
    inverse = 1.0 / total
    weights = (probs * inverse).astype(BF)
    fresh_weight = (fresh_prob * inverse).astype(BF).astype(F32)
    mixed = jnp.dot(weights, values, preferred_element_type=F32) + fresh_weight * new_value
    return mixed[:16, :HS].astype(BF), mixed[16:, HS:].astype(BF)


def layer_kernel(
    lengths, queries, new_keys, new_values, key_hbm, value_hbm,
    res, gain, wo_hbm, wg_hbm, wu_hbm, wd_hbm,
    out,
    keys, values, att, wo, wg, wu, wd,
    seen, wide, part, part_bf, quarter_in, hidden, scaled,
    squares_mine, squares, squares_in, squares_all,
    pa, pa_in1, pa_in2, za, za_in,
    pb, pb_in, xb, xb_in, scale_rows,
    act_a, act_b, down, down_bf, down_in, fin, send1, send1_bf, mid, mid_wide, send2, final, final_wide,
    csem, wsem, ss, rs,
):
    dp = lax.axis_index("dp")
    h = lax.axis_index("head")
    s = lax.axis_index("side")
    z = lax.rem(dp, 8)
    xy = dp // 8
    yh = lax.rem(xy, 2)
    x = xy // 2
    mine = 2 * s + h

    def dev(dx=0, dy=0, dz=0, dh=0, ds=0):
        nx = lax.rem(x + (dx + 4), 4)
        ny = lax.rem(yh + dy, 2)
        nz = lax.rem(z + (dz + 8), 8)
        return ((nx * 2 + ny) * 8 + nz, lax.rem(h + dh, 2), lax.rem(s + ds, 2))

    counter = [0]
    pending = []

    def ids(count):
        first = counter[0]
        counter[0] += count
        return first

    def when(condition, action):
        if condition is None:
            action()
        else:
            pl.when(condition)(action)

    def copy_of(src, dst, target, send_index, recv_index):
        return pltpu.make_async_remote_copy(
            src_ref=src, dst_ref=dst, send_sem=ss.at[send_index], recv_sem=rs.at[recv_index],
            device_id=target, device_id_type=MESH,
        )

    def send(src, dst, target, index, condition=None, slot=None):
        when(condition, copy_of(src, dst, target, index, index if slot is None else slot).start)
        pending.append((src, index, condition))

    def arrived(ref, index):
        copy_of(ref, ref, dev(dh=1), index, index).wait_recv()

    caches = []
    for r in range(3):
        for k, (src, dst) in enumerate(((key_hbm, keys), (value_hbm, values))):
            copy = pltpu.make_async_copy(src.at[r], dst.at[r], csem.at[2 * r + k])
            copy.start()
            caches.append(copy)

    plane = [(dx, dy) for dx in range(4) for dy in range(2)]
    peers = [dict(dx=dx, dy=dy, dh=dh) for dx, dy in plane for dh in range(2) if dx or dy or dh]
    peers += [dict(dz=dz) for dz in range(1, 8)]
    peers += [dict(dy=dy, dh=dh, ds=1) for dy in range(2) for dh in range(2)]
    barrier = pltpu.get_barrier_semaphore()
    for peer in peers:
        pl.semaphore_signal(barrier, inc=1, device_id=dev(**peer), device_id_type=MESH)

    loads = []

    def load(src, dst):
        copy = pltpu.make_async_copy(src, dst, wsem.at[len(loads)])
        copy.start()
        loads.append(copy)

    units = pl.ds(pl.multiple_of(UNITS * yh, 128), UNITS)
    others = pl.ds(pl.multiple_of(UNITS * (1 - yh), 128), UNITS)
    w_id = ids(7)
    cuts = [(u, 128 * NA, 128 * NB) for u in range(2)]
    cuts += [(u, 64 * NA * k, 64 * NA) for u in range(2) for k in range(2)]
    pieces = [
        (
            (wg_hbm, wu_hbm)[u].at[:, pl.ds(pl.multiple_of(UNITS * (1 - yh) + first, 128), count)],
            (wg, wu)[u].at[yh, :, pl.ds(first, count)],
        )
        for u, first, count in cuts
    ]
    pushed = [0]

    def push(count):
        for _ in range(count):
            src, dst = pieces[pushed[0]]
            send(src, dst, dev(dy=1), w_id + pushed[0])
            pushed[0] += 1

    for r in range(3):
        q = queries[...].astype(F32)[r : r + 1]
        q = jnp.concatenate([q[:, HS * g : HS * g + HS] for g in range(32)], axis=0)
        caches[2 * r].wait()
        caches[2 * r + 1].wait()
        if r == 0:
            pl.semaphore_wait(barrier, len(peers))
            push(PUSH[0])
        if r == 2:
            load(wo_hbm, wo)
            load(wg_hbm.at[:, units], wg.at[yh])
            load(wu_hbm.at[:, units], wu.at[yh])
            load(wd_hbm.at[units], wd.at[yh])
        low, high = attend_row(
            lengths[0, r], q, new_keys[...].astype(F32)[r : r + 1], new_values[...].astype(F32)[r : r + 1],
            keys[r], values[r],
        )
        att[r, 0] = low
        att[r, 1] = high

    y_id = ids(4)
    for ny in range(2):
        for ns in range(2):
            if ny or ns:
                head = s if ns == 0 else 1 - s
                send(att.at[:, head], seen.at[s, dp], dev(dy=ny, ds=ns), y_id + 2 * ny + ns)
    seen[s, dp] = att[:, s]

    za_id = ids(8)
    xa_id = ids(8 * 3)
    xyb_id = ids(8)
    zb_id = ids(16)

    def slot(nx, ny, nz):
        return (nx * 2 + ny) * 8 + nz

    xs = [lax.rem(x + d, 4) for d in range(4)]
    zs = [lax.rem(z + d, 8) for d in range(8)]
    ys = [yh, 1 - yh]

    arrived(seen.at[1 - s, dp], y_id + 1)
    there = slot(x, ys[1], z)
    arrived(seen.at[s, there], y_id + 2)
    arrived(seen.at[1 - s, there], y_id + 3)

    push(PUSH[1])

    seen8 = seen.at[0].reshape(4, 2, 8, 3, 16, HS)

    def pair_ref(nx, nz):
        return seen8.at[nx, :, nz]

    for d in range(1, 8):
        send(pair_ref(x, z), pair_ref(x, z), dev(dz=d), za_id + d)
    for j in range(1, 4):
        send(pair_ref(x, z), pair_ref(x, z), dev(dx=j), xa_id + j - 1)

    seenx = seen.at[1].reshape(4, 2, 8, 3, 16, HS)
    for j in range(1, 4):
        send(seenx.at[x, :, z], seenx.at[x, :, z], dev(dx=j), xyb_id + j)
    for j in range(1, 4):
        arrived(seenx.at[lax.rem(x + 4 - j, 4), :, z], xyb_id + j)
    seenz = seen.at[1].reshape(8, 8, 3, 16, HS)

    def ring(step, towards, which):
        return seenz.at[pl.ds(4 * which, 4), lax.rem(z + 8 - towards * (step - 1), 8)]

    def ring_id(step, towards, which):
        return zb_id + step * 4 + 2 * which + (0 if towards > 0 else 1)

    def last(towards):
        return 0 if towards > 0 else 1

    for which in range(2):
        for t in (1, -1):
            send(ring(1, t, which), ring(1, t, which), dev(dz=t), ring_id(0, t, which))

    plan = {1: (1, 7), 2: (2, 6), 3: (3, 5), 4: (4,)}
    for step in range(1, 5):
        for d in plan[step]:
            nz = zs[8 - d]
            arrived(pair_ref(x, nz), za_id + d)
            for j in range(1, 4):
                send(pair_ref(x, nz), pair_ref(x, nz), dev(dx=j), xa_id + 3 * d + j - 1)
        for which in range(2):
            for t in (1, -1):
                if step == 4 and which != last(t):
                    continue
                arrived(ring(step + 1, t, which), ring_id(step - 1, t, which))
                if step < 3 or (step == 3 and which == last(t)):
                    send(ring(step + 1, t, which), ring(step + 1, t, which), dev(dz=t), ring_id(step, t, which))

    loads[0].wait()

    def project(m):
        wide[...] = seen[m].reshape(64 * 3 * 16, HS).astype(F32)
        total = jnp.zeros((192, 256), F32)
        for g in range(8):
            left_half = wide[pl.ds(2 * g, 192, stride=16), :]
            right_half = wide[pl.ds(2 * g + 1, 192, stride=16), :]
            piece = jnp.concatenate([left_half, right_half], axis=1).astype(BF)
            total = total + jnp.dot(piece, wo[256 * g : 256 * g + 256, :], preferred_element_type=F32)
        for k in range(2):
            part[2 * m + k] = total[96 * k : 96 * k + 96]
            part_bf[2 * m + k] = total[96 * k : 96 * k + 96].astype(BF)

    project(1)
    for d in range(8):
        nz = lax.rem(z + 8 - d, 8)
        for j in range(1, 4):
            arrived(pair_ref(lax.rem(x + 4 - j, 4), nz), xa_id + 3 * d + j - 1)
    project(0)

    group = [(1, 0), (0, 1), (1, 1)]
    q1 = ids(3)
    for k, (dh, ds) in enumerate(group):
        there = 2 * lax.rem(s + ds, 2) + lax.rem(h + dh, 2)
        send(part_bf.at[there], quarter_in.at[k], dev(dh=dh, ds=ds), q1 + k)
    total = res[mine].astype(F32) + part[mine]
    for k in range(3):
        arrived(quarter_in.at[k], q1 + k)
        total = total + quarter_in[k].astype(F32)
    hidden[...] = total
    scaled[yh, mine] = (total * gain[...].reshape(1, 256).astype(F32)).astype(BF)
    group8 = [(dy, dh, ds) for dy in range(2) for dh in range(2) for ds in range(2)][1:]
    q2 = ids(7)

    def quarter(dh, ds):
        return 2 * lax.rem(s + ds, 2) + lax.rem(h + dh, 2)

    for k, (dy, dh, ds) in enumerate(group8):
        send(scaled.at[yh, mine], scaled.at[yh, mine], dev(dy=dy, dh=dh, ds=ds), q2 + k)

    row_square = jnp.sum(total * total, axis=1, keepdims=True)
    diagonal = lax.broadcasted_iota(jnp.int32, (96, 128), 0) == lax.broadcasted_iota(jnp.int32, (96, 128), 1)
    lanes = jnp.sum(jnp.where(diagonal, row_square, 0.0), axis=0, keepdims=True)
    squares_mine[yh, mine] = jnp.broadcast_to(lanes, (8, 128))
    sg, sx, sz = ids(7), ids(3), ids(7)
    for k, (dy, dh, ds) in enumerate(group8):
        send(squares_mine.at[yh, mine], squares_mine.at[yh, mine], dev(dy=dy, dh=dh, ds=ds), sg + k)

    def squares_x():
        for k, (dy, dh, ds) in enumerate(group8):
            arrived(squares_mine.at[ys[dy], quarter(dh, ds)], sg + k)
        row = lax.broadcasted_iota(jnp.int32, (8, 128), 0)
        value = jnp.zeros((8, 128), F32)
        for k in range(4):
            value = value + jnp.where(row == k, squares_mine[0, k] + squares_mine[1, k], 0.0)
        squares[0] = value
        for j in range(1, 4):
            send(squares.at[0], squares_in.at[j - 1], dev(dx=j), sx + j - 1)

    def squares_z():
        for j in range(3):
            arrived(squares_in.at[j], sx + j)
        squares[1] = squares[0] + squares_in[0] + squares_in[1] + squares_in[2]
        for d in range(1, 8):
            send(squares.at[1], squares_in.at[2 + d], dev(dz=d), sz + d - 1)

    def squares_done():
        value = squares[1]
        for d in range(1, 8):
            arrived(squares_in.at[2 + d], sz + d - 1)
            value = value + squares_in[2 + d]
        squares_all[...] = lax.rsqrt(value / D + 1e-05)

    for k, (dy, dh, ds) in enumerate(group8):
        arrived(scaled.at[ys[dy], quarter(dh, ds)], q2 + k)

    rows = jnp.concatenate([scaled[0].reshape(384, 256), scaled[1].reshape(384, 256)], axis=1)
    xa1, xa2, xa3 = ids(8), ids(8), ids(8)
    zb = ids(16)
    zra = ids(16)
    xyr = ids(6)
    weight = (wg, wu)
    back = [lax.rem(x + 4 - d, 4) for d in range(4)]
    def multiply(u, c, count):
        columns = weight[u][:, :, 128 * c : 128 * (c + count)].reshape(512, 128 * count)
        value = jnp.dot(rows, columns, preferred_element_type=F32).astype(BF)
        return [value[:, 128 * i : 128 * i + 128] for i in range(count)]

    def group_of(g):
        return g // 2, pl.ds(4 * (g % 2), 4)

    def multiply_a(g):
        u, some = group_of(g)
        for c in range(4 * (g % 2), 4 * (g % 2) + 4, 2):
            for i, value in enumerate(multiply(u, c, 2)):
                pa[u, :, :, c + i] = value.reshape(4, 2, 48, 128)
        send(pa.at[u, xs[2], 0, some], pa_in1.at[u, 0, some], dev(dx=1), xa1 + 2 * g)
        send(pa.at[u, xs[2], 1, some], pa_in1.at[u, 1, some], dev(dx=-1), xa1 + 2 * g + 1)
        send(pa.at[u, xs[1], 1, some], pa_in2.at[u, 0, 1, some], dev(dx=1), xa2 + 2 * g)
        send(pa.at[u, xs[3], 0, some], pa_in2.at[u, 1, 0, some], dev(dx=-1), xa2 + 2 * g + 1)

    def half(towards):
        return pl.ds(0 if towards > 0 else FLAT // 2, FLAT // 2)

    def z_block(u, dist, towards):
        there = lax.rem(z + 8 + towards * dist, 8)
        if dist == 4:
            return pb.at[u, there, half(towards)]
        return pb.at[u, there]

    def z_in(u, dist, towards):
        dst = pb_in.at[u, 0 if towards > 0 else 1, dist - 1]
        if dist == 4:
            return dst.at[half(towards)]
        return dst

    def z_id(u, dist, towards):
        return zb + 8 * u + 2 * (dist - 1) + (0 if towards > 0 else 1)

    def z_send(u, dist):
        for t in (1, -1):
            send(z_block(u, dist, t), z_in(u, dist, t), dev(dz=t), z_id(u, dist, t))

    def multiply_b(u):
        for c in range(0, NB, 2):
            for i, value in enumerate(multiply(u, NA + c, min(2, NB - c))):
                pb[u, :, 48 * (c + i) : 48 * (c + i) + 48] = value.reshape(8, 48, 128)
        pb[u, :, 48 * NB :] = jnp.zeros((8, FLAT - 48 * NB, 128), BF)
        z_send(u, 4)

    def z_step(u, dist):
        for t in (1, -1):
            arrived(z_in(u, dist, t), z_id(u, dist, t))
            there = lax.rem(z + 8 + t * (dist - 1), 8)
            d = 0 if t > 0 else 1
            part_rows = half(t) if dist == 4 else pl.ds(0, FLAT)
            pb[u, there, part_rows] = (
                pb[u, there, part_rows].astype(F32) + pb_in[u, d, dist - 1, part_rows].astype(F32)
            ).astype(BF)
        z_send(u, dist - 1)

    def x_step(g):
        u, some = group_of(g)
        for k, there in enumerate((xs[1], xs[3])):
            arrived(pa_in1.at[u, k, some], xa1 + 2 * g + k)
            pa[u, there, k, some] = (pa[u, there, k, some].astype(F32) + pa_in1[u, k, some].astype(F32)).astype(BF)
            send(pa.at[u, there, k, some], pa_in2.at[u, k, k, some], dev(dx=1 - 2 * k), xa3 + 2 * g + k)

    def x_done(g):
        u, some = group_of(g)
        arrived(pa_in2.at[u, 0, 1, some], xa2 + 2 * g)
        arrived(pa_in2.at[u, 1, 0, some], xa2 + 2 * g + 1)
        arrived(pa_in2.at[u, 0, 0, some], xa3 + 2 * g)
        arrived(pa_in2.at[u, 1, 1, some], xa3 + 2 * g + 1)
        for k in range(2):
            za[u, k, some] = (
                pa[u, x, k, some].astype(F32) + pa_in2[u, 0, k, some].astype(F32) + pa_in2[u, 1, k, some].astype(F32)
            ).astype(BF)
        for c in range(4 * (g % 2), 4 * (g % 2) + 4):
            places = lax.rem(c - z + 8, 8)
            send(
                za.at[u, :, c], za_in.at[u, places], (xy * 8 + c, h, s), zra + 8 * u + c, z != c,
                slot=zra + 8 * u + places,
            )

    def own_flat(nx):
        return pl.ds(pl.multiple_of(FLAT // 4 * nx, FLAT // 4), FLAT // 4)

    def xb_start(u):
        for t in (1, -1):
            arrived(z_in(u, 1, t), z_id(u, 1, t))
        xb[u] = (
            pb[u, z].astype(F32) + pb_in[u, 0, 0].astype(F32) + pb_in[u, 1, 0].astype(F32)
        ).astype(BF)
        for j in range(1, 4):
            send(xb.at[u, own_flat(xs[j])], xb_in.at[u, j - 1], dev(dx=j), xyr + 3 * u + j - 1)

    squares_x()
    push(PUSH[2])
    loads[1].wait()
    loads[2].wait()
    def weights_there(*numbers):
        for k in numbers:
            u, first, count = cuts[k]
            arrived(weight[u].at[1 - yh, :, pl.ds(first, count)], w_id + k)

    for u in range(2):
        weights_there(u)
        multiply_b(u)
    for g in range(2):
        weights_there(2 + g)
        multiply_a(g)
    z_step(0, 4)
    z_step(1, 4)
    weights_there(4)
    multiply_a(2)
    x_step(0)
    x_step(1)
    z_step(0, 3)
    z_step(1, 3)
    weights_there(5)
    multiply_a(3)
    send(wd_hbm.at[others], wd.at[yh], dev(dy=1), w_id + 6)
    squares_z()
    x_step(2)
    x_done(0)
    x_done(1)
    z_step(0, 2)
    x_step(3)
    z_step(1, 2)
    x_done(2)
    squares_done()
    x_done(3)
    xb_start(0)
    xb_start(1)

    def scaling(index, offset, count):
        lane_scale = squares_all[pl.ds(index, 1)]
        pick = (
            lax.broadcasted_iota(jnp.int32, (count, 128), 0) + offset
            == lax.broadcasted_iota(jnp.int32, (count, 128), 1)
        )
        return jnp.sum(jnp.where(pick, lane_scale, 0.0), axis=1, keepdims=True)

    def activate(gate, upper, scale):
        gate = gate * scale
        return (gate / (1.0 + jnp.exp(-gate)) * (upper * scale)).astype(BF)

    ga, gax = ids(8), ids(24)
    gb, gbz = ids(4), ids(8)

    scale_rows[...] = jnp.broadcast_to(scaling(z // 2, 48 * lax.rem(z, 2), 48), (48, 128)).reshape(3, 16, 128)
    sums = []
    for u in range(2):
        value = xb[u, own_flat(x)].astype(F32)
        for j in range(3):
            arrived(xb_in.at[u, j], xyr + 3 * u + j)
            value = value + xb_in[u, j].astype(F32)
        sums.append(value)
    tiles = [scale_rows[lax.rem(4 * x + i, 3)] for i in range(4)]
    act_b[z, own_flat(x)] = activate(sums[0], sums[1], jnp.concatenate(tiles, axis=0))
    for j in range(1, 4):
        send(act_b.at[z, own_flat(x)], act_b.at[z, own_flat(x)], dev(dx=j), gb + j)

    sums = []
    for u in range(2):
        value = za[u, :, z].astype(F32)
        for d in range(1, 8):
            arrived(za_in.at[u, d], zra + 8 * u + d)
            value = value + za_in[u, d].astype(F32)
        sums.append(value.reshape(96, 128))
    act_a[x, z] = activate(sums[0], sums[1], scaling(x, 0, 96))
    for d in range(1, 8):
        send(act_a.at[x, z], act_a.at[x, z], dev(dz=d), ga + d)
    for j in range(1, 4):
        send(act_a.at[x, z], act_a.at[x, z], dev(dx=j), gax + j - 1)

    for j in range(1, 4):
        arrived(act_b.at[z, own_flat(back[j])], gb + j)

    def gz_id(dist, towards):
        return gbz + 2 * (dist - 1) + (0 if towards > 0 else 1)

    for t in (1, -1):
        for dist in (2, 1):
            send(act_b.at[z], act_b.at[z], dev(dz=t * dist), gz_id(dist, t))

    def a_step(d):
        nz = zs[(8 - d) % 8]
        arrived(act_a.at[x, nz], ga + d)
        for j in range(1, 4):
            send(act_a.at[x, nz], act_a.at[x, nz], dev(dx=j), gax + 3 * d + j - 1)

    a_step(1)
    a_step(7)
    for t in (1, -1):
        far = act_b.at[zs[(8 - 2 * t) % 8]]
        arrived(far, gz_id(2, t))
        send(far, far, dev(dz=t), gz_id(3, t))
        send(far.at[half(t)], far.at[half(t)], dev(dz=2 * t), gz_id(4, t))
    for d in (2, 6, 3, 5, 4):
        a_step(d)
    for t in (1, -1):
        arrived(act_b.at[zs[(8 - t) % 8]], gz_id(1, t))
        arrived(act_b.at[zs[(8 - 3 * t) % 8]], gz_id(3, t))
        arrived(act_b.at[zs[4], half(t)], gz_id(4, t))

    loads[3].wait()
    arrived(wd.at[1 - yh], w_id + 6)

    def lower(chunks, first):
        for i in range(0, len(chunks), 2):
            pieces, numbers = zip(*chunks[i : i + 2])
            piece = jnp.concatenate(pieces, axis=1) if len(pieces) == 2 else pieces[0]
            depth = pl.ds(128 * numbers[0], 128 * len(numbers))
            for ny in range(2):
                value = jnp.dot(piece, wd[ny, depth], preferred_element_type=F32).reshape(4, 96, 256)
                if first and i == 0:
                    down[ny] = value
                else:
                    down[ny] += value

    lower([(act_b[:, 48 * c : 48 * c + 48].reshape(384, 128), NA + c) for c in range(NB)], True)
    for d in range(8):
        for j in range(1, 4):
            arrived(act_a.at[back[j], zs[(8 - d) % 8]], gax + 3 * d + j - 1)
    lower([(act_a[:, c].reshape(384, 128), c) for c in range(NA)], False)
    down_bf[...] = down[...].astype(BF)

    q3 = ids(7)
    for k, (dy, dh, ds) in enumerate(group8):
        send(down_bf.at[ys[dy], quarter(dh, ds)], down_in.at[k], dev(dy=dy, dh=dh, ds=ds), q3 + k)
    total = hidden[...] + down[yh, mine]
    for k in range(7):
        arrived(down_in.at[k], q3 + k)
        total = total + down_in[k].astype(F32)
    fin[0] = total[:, :128]
    fin[1] = total[:, 128:]

    for r in range(3):
        for j in range(2):
            value = fin[j, pl.ds(r, 32, stride=3), :]
            for k in range(4):
                send1[pl.ds((2 * r + j) * 4 + k, 8, stride=32), :] = value[8 * k : 8 * k + 8]
    for k in range(8):
        send1[pl.ds(24 + k, 8, stride=32), :] = jnp.zeros((8, 128), F32)
    send1_bf[...] = send1[...].astype(BF).reshape(8, 32, 128)
    f1 = ids(7)
    for d in range(1, 8):
        send(send1_bf.at[zs[d]], mid.at[z], dev(dz=d), f1 + d - 1)
    mid[z] = send1_bf[z]
    for d in range(1, 8):
        arrived(mid.at[zs[8 - d]], f1 + d - 1)
    mid_wide[...] = mid[...].astype(F32).reshape(256, 128)
    for k in range(4):
        rows_k = [mid_wide[pl.ds(4 * i + k, 8, stride=32), :] for i in range(6)]
        send2[k] = jnp.concatenate(rows_k, axis=0).astype(BF)

    f2 = ids(16)
    for xl in range(2):
        for ny in range(2):
            for nh in range(2):
                nx = 2 * h + xl
                own = (nx == x) & (ny == yh) & (nh == h)

                @pl.when(own)
                def _():
                    final[xy] = send2[2 * xl + ny]

                send(
                    send2.at[2 * xl + ny], final.at[xy], ((nx * 2 + ny) * 8 + z, nh, s),
                    f2 + 4 * xl + 2 * ny + nh, jnp.logical_not(own), slot=f2 + xy,
                )
    for k in range(8):
        own = (xy == k) & (h == x // 2)

        @pl.when(jnp.logical_not(own))
        def _():
            arrived(final.at[k], f2 + k)

    final_wide[...] = final[...].astype(F32).reshape(384, 128)
    for k in range(8):
        columns = [final_wide[pl.ds(48 * k + 8 * j + i, 3, stride=16), :] for i in range(8) for j in range(2)]
        out[:, 2048 * k : 2048 * k + 2048] = jnp.concatenate(columns, axis=1).astype(BF)

    for ref, index, condition in pending:
        when(condition, lambda: copy_of(ref, ref, dev(dh=1), index, index).wait_send())
    assert counter[0] <= SEMS


SEMS = 320


def layer(
    lengths, queries, new_keys, new_values, key_cache, value_cache,
    residual, gain, out_weight, gate_weight, up_weight, down_weight,
):
    vmem = pl.BlockSpec(memory_space=pltpu.VMEM)
    anywhere = pl.BlockSpec(memory_space=pl.ANY)
    scratch = [
        pltpu.VMEM((3, 2048, 256), BF),
        pltpu.VMEM((3, 2048, 256), BF),
        pltpu.VMEM((3, 2, 16, HS), BF),
        pltpu.VMEM((2048, 256), BF),
        pltpu.VMEM((2, 256, UNITS), BF),
        pltpu.VMEM((2, 256, UNITS), BF),
        pltpu.VMEM((2, UNITS, 256), BF),
        pltpu.VMEM((2, 64, 3, 16, HS), BF),
        pltpu.VMEM((64 * 3 * 16, HS), F32),
        pltpu.VMEM((4, 96, 256), F32),
        pltpu.VMEM((4, 96, 256), BF),
        pltpu.VMEM((3, 96, 256), BF),
        pltpu.VMEM((96, 256), F32),
        pltpu.VMEM((2, 4, 96, 256), BF),
        pltpu.VMEM((2, 4, 8, 128), F32),
        pltpu.VMEM((2, 8, 128), F32),
        pltpu.VMEM((10, 8, 128), F32),
        pltpu.VMEM((8, 128), F32),
        pltpu.VMEM((2, 4, 2, NA, 48, 128), BF),
        pltpu.VMEM((2, 2, NA, 48, 128), BF),
        pltpu.VMEM((2, 2, 2, NA, 48, 128), BF),
        pltpu.VMEM((2, 2, NA, 48, 128), BF),
        pltpu.VMEM((2, 8, 2, 48, 128), BF),
        pltpu.VMEM((2, 8, FLAT, 128), BF),
        pltpu.VMEM((2, 2, 4, FLAT, 128), BF),
        pltpu.VMEM((2, FLAT, 128), BF),
        pltpu.VMEM((2, 3, FLAT // 4, 128), BF),
        pltpu.VMEM((3, 16, 128), F32),
        pltpu.VMEM((4, NA, 96, 128), BF),
        pltpu.VMEM((8, FLAT, 128), BF),
        pltpu.VMEM((2, 4, 96, 256), F32),
        pltpu.VMEM((2, 4, 96, 256), BF),
        pltpu.VMEM((7, 96, 256), BF),
        pltpu.VMEM((2, 96, 128), F32),
        pltpu.VMEM((256, 128), F32),
        pltpu.VMEM((8, 32, 128), BF),
        pltpu.VMEM((8, 32, 128), BF),
        pltpu.VMEM((256, 128), F32),
        pltpu.VMEM((4, 48, 128), BF),
        pltpu.VMEM((8, 48, 128), BF),
        pltpu.VMEM((384, 128), F32),
        pltpu.SemaphoreType.DMA((6,)),
        pltpu.SemaphoreType.DMA((4,)),
        pltpu.SemaphoreType.DMA((SEMS,)),
        pltpu.SemaphoreType.DMA((SEMS,)),
    ]
    return pl.pallas_call(
        layer_kernel,
        out_shape=jax.ShapeDtypeStruct((3, D), BF),
        in_specs=[pl.BlockSpec(memory_space=pltpu.SMEM), vmem, vmem, vmem, anywhere, anywhere, vmem, vmem] + [anywhere] * 4,
        out_specs=vmem,
        scratch_shapes=scratch,
        compiler_params=pltpu.CompilerParams(collective_id=0, has_side_effects=True, vmem_limit_bytes=VMEM_LIMIT),
        cost_estimate=pl.CostEstimate(flops=2 * 384 * 256 * 12032, bytes_accessed=8 * 2**20, transcendentals=0),
        name="layer",
    )(lengths, queries, new_keys, new_values, key_cache, value_cache, residual.reshape(4, 96, 256), gain, out_weight, gate_weight, up_weight, down_weight)


def body(
    queries,
    new_keys,
    new_values,
    key_cache,
    value_cache,
    cache_lengths,
    residual,
    norm_gain,
    out_weight,
    gate_weight,
    up_weight,
    down_weight,
):
    rows = layer(
        cache_lengths, queries[0], new_keys[0], new_values[0], key_cache[0], value_cache[0],
        residual, norm_gain, out_weight, gate_weight, up_weight, down_weight,
    )
    return rows.reshape(1, 3, D)


def solution(mesh):
    return jax.shard_map(
        body,
        mesh=mesh,
        in_specs=(
            P("side", "dp", "head"),
            P("side", "dp", "head"),
            P("side", "dp", "head"),
            P("side", "dp", None, "head"),
            P("side", "dp", None, "head"),
            P("side", "dp"),
            P(None, None, "dp"),
            P("dp"),
            P(("head", "side"), "dp"),
            P("dp", ("head", "side")),
            P("dp", ("head", "side")),
            P(("head", "side"), "dp"),
        ),
        out_specs=P("side", "dp", None),
        check_vma=False,
    )
```

```python
import math

import jax
import jax.numpy as jnp
from jax import lax
from jax.experimental import pallas as pl
from jax.experimental.pallas import tpu as pltpu
from jax.sharding import PartitionSpec as P

D = 16384
HS = 128
BF = jnp.bfloat16
F32 = jnp.float32
MESH = pl.DeviceIdType.MESH
VMEM_LIMIT = 56 * 2**20

UNITS = 1664
NA = 8
NB = 5
PUSH = (1, 4, 2)
FLAT = 256


def attend_row(length, q, new_key, new_value, keys, values):
    span = keys.shape[0]
    zero = jnp.zeros((16, HS), F32)
    wide = jnp.concatenate(
        [jnp.concatenate([q[:16], zero], axis=1), jnp.concatenate([zero, q[16:]], axis=1)], axis=0
    )
    scale = 1.0 / math.sqrt(HS)
    nt = (((1,), (1,)), ((), ()))
    scores = lax.dot_general(wide.astype(BF), keys, nt, preferred_element_type=F32) * scale
    fresh = jnp.sum(wide * new_key, axis=1, keepdims=True) * scale
    valid = lax.broadcasted_iota(jnp.int32, (32, span), 1) < length
    masked = jnp.where(valid, scores, -jnp.inf)
    highest = jnp.maximum(jnp.max(masked, axis=1, keepdims=True), fresh)
    probs = jnp.exp(masked - highest)
    fresh_prob = jnp.exp(fresh - highest)
    total = jnp.sum(probs, axis=1, keepdims=True) + fresh_prob
    inverse = 1.0 / total
    weights = (probs * inverse).astype(BF)
    fresh_weight = (fresh_prob * inverse).astype(BF).astype(F32)
    mixed = jnp.dot(weights, values, preferred_element_type=F32) + fresh_weight * new_value
    return mixed[:16, :HS].astype(BF), mixed[16:, HS:].astype(BF)


def layer_kernel(
    lengths, queries, new_keys, new_values, key_hbm, value_hbm,
    res, gain, wo_hbm, wg_hbm, wu_hbm, wd_hbm,
    out,
    keys, values, att, wo, wg, wu, wd,
    seen, wide, part, part_bf, quarter_in, hidden, scaled,
    squares_mine, squares, squares_in, squares_all,
    pa, pa_in1, pa_in2, za, za_in,
    pb, pb_in, xb, xb_in, scale_rows,
    act_a, act_b, down, down_bf, down_in, fin, send1, send1_bf, mid, mid_wide, send2, final, final_wide,
    csem, wsem, ss, rs,
):
    dp = lax.axis_index("dp")
    h = lax.axis_index("head")
    s = lax.axis_index("side")
    z = lax.rem(dp, 8)
    xy = dp // 8
    yh = lax.rem(xy, 2)
    x = xy // 2
    mine = 2 * s + h

    def dev(dx=0, dy=0, dz=0, dh=0, ds=0):
        nx = lax.rem(x + (dx + 4), 4)
        ny = lax.rem(yh + dy, 2)
        nz = lax.rem(z + (dz + 8), 8)
        return ((nx * 2 + ny) * 8 + nz, lax.rem(h + dh, 2), lax.rem(s + ds, 2))

    counter = [0]
    pending = []

    def ids(count):
        first = counter[0]
        counter[0] += count
        return first

    def when(condition, action):
        if condition is None:
            action()
        else:
            pl.when(condition)(action)

    def copy_of(src, dst, target, send_index, recv_index):
        return pltpu.make_async_remote_copy(
            src_ref=src, dst_ref=dst, send_sem=ss.at[send_index], recv_sem=rs.at[recv_index],
            device_id=target, device_id_type=MESH,
        )

    def send(src, dst, target, index, condition=None, slot=None):
        when(condition, copy_of(src, dst, target, index, index if slot is None else slot).start)
        pending.append((src, index, condition))

    def arrived(ref, index):
        copy_of(ref, ref, dev(dh=1), index, index).wait_recv()

    caches = []
    for r in range(3):
        for k, (src, dst) in enumerate(((key_hbm, keys), (value_hbm, values))):
            copy = pltpu.make_async_copy(src.at[r], dst.at[r], csem.at[2 * r + k])
            copy.start()
            caches.append(copy)

    plane = [(dx, dy) for dx in range(4) for dy in range(2)]
    peers = [dict(dx=dx, dy=dy, dh=dh) for dx, dy in plane for dh in range(2) if dx or dy or dh]
    peers += [dict(dz=dz) for dz in range(1, 8)]
    peers += [dict(dy=dy, dh=dh, ds=1) for dy in range(2) for dh in range(2)]
    barrier = pltpu.get_barrier_semaphore()
    for peer in peers:
        pl.semaphore_signal(barrier, inc=1, device_id=dev(**peer), device_id_type=MESH)

    loads = []

    def load(src, dst):
        copy = pltpu.make_async_copy(src, dst, wsem.at[len(loads)])
        copy.start()
        loads.append(copy)

    units = pl.ds(pl.multiple_of(UNITS * yh, 128), UNITS)
    others = pl.ds(pl.multiple_of(UNITS * (1 - yh), 128), UNITS)
    w_id = ids(8)
    cuts = [(0, 128 * NA, 256), (0, 128 * NA + 256, 128 * NB - 256), (1, 128 * NA, 128 * NB)]
    cuts += [(u, 64 * NA * k, 64 * NA) for u in range(2) for k in range(2)]
    pieces = [
        (
            (wg_hbm, wu_hbm)[u].at[:, pl.ds(pl.multiple_of(UNITS * (1 - yh) + first, 128), count)],
            (wg, wu)[u].at[yh, :, pl.ds(first, count)],
        )
        for u, first, count in cuts
    ]
    pushed = [0]

    def push(count):
        for _ in range(count):
            src, dst = pieces[pushed[0]]
            send(src, dst, dev(dy=1), w_id + pushed[0])
            pushed[0] += 1

    for r in range(3):
        q = queries[...].astype(F32)[r : r + 1]
        q = jnp.concatenate([q[:, HS * g : HS * g + HS] for g in range(32)], axis=0)
        caches[2 * r].wait()
        caches[2 * r + 1].wait()
        if r == 0:
            pl.semaphore_wait(barrier, len(peers))
            push(PUSH[0])
        if r == 2:
            load(wo_hbm, wo)
            load(wg_hbm.at[:, units], wg.at[yh])
            load(wu_hbm.at[:, units], wu.at[yh])
            load(wd_hbm.at[units], wd.at[yh])
        low, high = attend_row(
            lengths[0, r], q, new_keys[...].astype(F32)[r : r + 1], new_values[...].astype(F32)[r : r + 1],
            keys[r], values[r],
        )
        att[r, 0] = low
        att[r, 1] = high

    y_id = ids(4)
    for ny in range(2):
        for ns in range(2):
            if ny or ns:
                head = s if ns == 0 else 1 - s
                send(att.at[:, head], seen.at[s, dp], dev(dy=ny, ds=ns), y_id + 2 * ny + ns)
    seen[s, dp] = att[:, s]

    za_id = ids(8)
    xa_id = ids(8 * 3)
    xyb_id = ids(8)
    zb_id = ids(16)

    def slot(nx, ny, nz):
        return (nx * 2 + ny) * 8 + nz

    xs = [lax.rem(x + d, 4) for d in range(4)]
    zs = [lax.rem(z + d, 8) for d in range(8)]
    ys = [yh, 1 - yh]

    arrived(seen.at[1 - s, dp], y_id + 1)
    there = slot(x, ys[1], z)
    arrived(seen.at[s, there], y_id + 2)
    arrived(seen.at[1 - s, there], y_id + 3)

    push(PUSH[1])

    seen8 = seen.at[0].reshape(4, 2, 8, 3, 16, HS)

    def pair_ref(nx, nz):
        return seen8.at[nx, :, nz]

    for d in range(1, 8):
        send(pair_ref(x, z), pair_ref(x, z), dev(dz=d), za_id + d)
    for j in range(1, 4):
        send(pair_ref(x, z), pair_ref(x, z), dev(dx=j), xa_id + j - 1)

    seenx = seen.at[1].reshape(4, 2, 8, 3, 16, HS)
    for j in range(1, 4):
        send(seenx.at[x, :, z], seenx.at[x, :, z], dev(dx=j), xyb_id + j)
    for j in range(1, 4):
        arrived(seenx.at[lax.rem(x + 4 - j, 4), :, z], xyb_id + j)
    seenz = seen.at[1].reshape(8, 8, 3, 16, HS)

    def ring(step, towards, which):
        return seenz.at[pl.ds(4 * which, 4), lax.rem(z + 8 - towards * (step - 1), 8)]

    def ring_id(step, towards, which):
        return zb_id + step * 4 + 2 * which + (0 if towards > 0 else 1)

    def last(towards):
        return 0 if towards > 0 else 1

    for which in range(2):
        for t in (1, -1):
            send(ring(1, t, which), ring(1, t, which), dev(dz=t), ring_id(0, t, which))

    plan = {1: (1, 7), 2: (2, 6), 3: (3, 5), 4: (4,)}
    for step in range(1, 5):
        for d in plan[step]:
            nz = zs[8 - d]
            arrived(pair_ref(x, nz), za_id + d)
            for j in range(1, 4):
                send(pair_ref(x, nz), pair_ref(x, nz), dev(dx=j), xa_id + 3 * d + j - 1)
        for which in range(2):
            for t in (1, -1):
                if step == 4 and which != last(t):
                    continue
                arrived(ring(step + 1, t, which), ring_id(step - 1, t, which))
                if step < 3 or (step == 3 and which == last(t)):
                    send(ring(step + 1, t, which), ring(step + 1, t, which), dev(dz=t), ring_id(step, t, which))

    loads[0].wait()

    def project(m):
        wide[...] = seen[m].reshape(64 * 3 * 16, HS).astype(F32)
        total = jnp.zeros((192, 256), F32)
        for g in range(8):
            left_half = wide[pl.ds(2 * g, 192, stride=16), :]
            right_half = wide[pl.ds(2 * g + 1, 192, stride=16), :]
            piece = jnp.concatenate([left_half, right_half], axis=1).astype(BF)
            total = total + jnp.dot(piece, wo[256 * g : 256 * g + 256, :], preferred_element_type=F32)
        for k in range(2):
            part[2 * m + k] = total[96 * k : 96 * k + 96]
            part_bf[2 * m + k] = total[96 * k : 96 * k + 96].astype(BF)

    project(1)
    for d in range(8):
        nz = lax.rem(z + 8 - d, 8)
        for j in range(1, 4):
            arrived(pair_ref(lax.rem(x + 4 - j, 4), nz), xa_id + 3 * d + j - 1)
    project(0)

    group = [(1, 0), (0, 1), (1, 1)]
    q1 = ids(3)
    for k, (dh, ds) in enumerate(group):
        there = 2 * lax.rem(s + ds, 2) + lax.rem(h + dh, 2)
        send(part_bf.at[there], quarter_in.at[k], dev(dh=dh, ds=ds), q1 + k)
    total = res[mine].astype(F32) + part[mine]
    for k in range(3):
        arrived(quarter_in.at[k], q1 + k)
        total = total + quarter_in[k].astype(F32)
    hidden[...] = total
    scaled[yh, mine] = (total * gain[...].reshape(1, 256).astype(F32)).astype(BF)
    group8 = [(dy, dh, ds) for dy in range(2) for dh in range(2) for ds in range(2)][1:]
    q2 = ids(7)

    def quarter(dh, ds):
        return 2 * lax.rem(s + ds, 2) + lax.rem(h + dh, 2)

    for k, (dy, dh, ds) in enumerate(group8):
        send(scaled.at[yh, mine], scaled.at[yh, mine], dev(dy=dy, dh=dh, ds=ds), q2 + k)

    row_square = jnp.sum(total * total, axis=1, keepdims=True)
    diagonal = lax.broadcasted_iota(jnp.int32, (96, 128), 0) == lax.broadcasted_iota(jnp.int32, (96, 128), 1)
    lanes = jnp.sum(jnp.where(diagonal, row_square, 0.0), axis=0, keepdims=True)
    squares_mine[yh, mine] = jnp.broadcast_to(lanes, (8, 128))
    sg, sx, sz = ids(7), ids(3), ids(7)
    for k, (dy, dh, ds) in enumerate(group8):
        send(squares_mine.at[yh, mine], squares_mine.at[yh, mine], dev(dy=dy, dh=dh, ds=ds), sg + k)

    def squares_x():
        for k, (dy, dh, ds) in enumerate(group8):
            arrived(squares_mine.at[ys[dy], quarter(dh, ds)], sg + k)
        row = lax.broadcasted_iota(jnp.int32, (8, 128), 0)
        value = jnp.zeros((8, 128), F32)
        for k in range(4):
            value = value + jnp.where(row == k, squares_mine[0, k] + squares_mine[1, k], 0.0)
        squares[0] = value
        for j in range(1, 4):
            send(squares.at[0], squares_in.at[j - 1], dev(dx=j), sx + j - 1)

    def squares_z():
        for j in range(3):
            arrived(squares_in.at[j], sx + j)
        squares[1] = squares[0] + squares_in[0] + squares_in[1] + squares_in[2]
        for d in range(1, 8):
            send(squares.at[1], squares_in.at[2 + d], dev(dz=d), sz + d - 1)

    def squares_done():
        value = squares[1]
        for d in range(1, 8):
            arrived(squares_in.at[2 + d], sz + d - 1)
            value = value + squares_in[2 + d]
        squares_all[...] = lax.rsqrt(value / D + 1e-05)

    for k, (dy, dh, ds) in enumerate(group8):
        arrived(scaled.at[ys[dy], quarter(dh, ds)], q2 + k)

    rows = jnp.concatenate([scaled[0].reshape(384, 256), scaled[1].reshape(384, 256)], axis=1)
    xa1, xa2, xa3 = ids(8), ids(8), ids(8)
    zb = ids(16)
    zra = ids(16)
    xyr = ids(6)
    weight = (wg, wu)
    back = [lax.rem(x + 4 - d, 4) for d in range(4)]
    def multiply(u, c, count):
        columns = weight[u][:, :, 128 * c : 128 * (c + count)].reshape(512, 128 * count)
        value = jnp.dot(rows, columns, preferred_element_type=F32).astype(BF)
        return [value[:, 128 * i : 128 * i + 128] for i in range(count)]

    def group_of(g):
        return g // 2, pl.ds(4 * (g % 2), 4)

    def multiply_a(g):
        u, some = group_of(g)
        for c in range(4 * (g % 2), 4 * (g % 2) + 4, 2):
            for i, value in enumerate(multiply(u, c, 2)):
                pa[u, :, :, c + i] = value.reshape(4, 2, 48, 128)
        send(pa.at[u, xs[2], 0, some], pa_in1.at[u, 0, some], dev(dx=1), xa1 + 2 * g)
        send(pa.at[u, xs[2], 1, some], pa_in1.at[u, 1, some], dev(dx=-1), xa1 + 2 * g + 1)
        send(pa.at[u, xs[1], 1, some], pa_in2.at[u, 0, 1, some], dev(dx=1), xa2 + 2 * g)
        send(pa.at[u, xs[3], 0, some], pa_in2.at[u, 1, 0, some], dev(dx=-1), xa2 + 2 * g + 1)

    def half(towards):
        return pl.ds(0 if towards > 0 else FLAT // 2, FLAT // 2)

    def z_block(u, dist, towards):
        there = lax.rem(z + 8 + towards * dist, 8)
        if dist == 4:
            return pb.at[u, there, half(towards)]
        return pb.at[u, there]

    def z_in(u, dist, towards):
        dst = pb_in.at[u, 0 if towards > 0 else 1, dist - 1]
        if dist == 4:
            return dst.at[half(towards)]
        return dst

    def z_id(u, dist, towards):
        return zb + 8 * u + 2 * (dist - 1) + (0 if towards > 0 else 1)

    def z_send(u, dist):
        for t in (1, -1):
            send(z_block(u, dist, t), z_in(u, dist, t), dev(dz=t), z_id(u, dist, t))

    def multiply_b(u):
        for c in range(0, NB, 2):
            for i, value in enumerate(multiply(u, NA + c, min(2, NB - c))):
                pb[u, :, 48 * (c + i) : 48 * (c + i) + 48] = value.reshape(8, 48, 128)
        pb[u, :, 48 * NB :] = jnp.zeros((8, FLAT - 48 * NB, 128), BF)
        z_send(u, 4)

    def z_step(u, dist):
        for t in (1, -1):
            arrived(z_in(u, dist, t), z_id(u, dist, t))
            there = lax.rem(z + 8 + t * (dist - 1), 8)
            d = 0 if t > 0 else 1
            part_rows = half(t) if dist == 4 else pl.ds(0, FLAT)
            pb[u, there, part_rows] = (
                pb[u, there, part_rows].astype(F32) + pb_in[u, d, dist - 1, part_rows].astype(F32)
            ).astype(BF)
        z_send(u, dist - 1)

    def x_step(g):
        u, some = group_of(g)
        for k, there in enumerate((xs[1], xs[3])):
            arrived(pa_in1.at[u, k, some], xa1 + 2 * g + k)
            pa[u, there, k, some] = (pa[u, there, k, some].astype(F32) + pa_in1[u, k, some].astype(F32)).astype(BF)
            send(pa.at[u, there, k, some], pa_in2.at[u, k, k, some], dev(dx=1 - 2 * k), xa3 + 2 * g + k)

    def x_done(g):
        u, some = group_of(g)
        arrived(pa_in2.at[u, 0, 1, some], xa2 + 2 * g)
        arrived(pa_in2.at[u, 1, 0, some], xa2 + 2 * g + 1)
        arrived(pa_in2.at[u, 0, 0, some], xa3 + 2 * g)
        arrived(pa_in2.at[u, 1, 1, some], xa3 + 2 * g + 1)
        for k in range(2):
            za[u, k, some] = (
                pa[u, x, k, some].astype(F32) + pa_in2[u, 0, k, some].astype(F32) + pa_in2[u, 1, k, some].astype(F32)
            ).astype(BF)
        for c in range(4 * (g % 2), 4 * (g % 2) + 4):
            places = lax.rem(c - z + 8, 8)
            send(
                za.at[u, :, c], za_in.at[u, places], (xy * 8 + c, h, s), zra + 8 * u + c, z != c,
                slot=zra + 8 * u + places,
            )

    def own_flat(nx):
        return pl.ds(pl.multiple_of(FLAT // 4 * nx, FLAT // 4), FLAT // 4)

    def xb_start(u):
        for t in (1, -1):
            arrived(z_in(u, 1, t), z_id(u, 1, t))
        xb[u] = (
            pb[u, z].astype(F32) + pb_in[u, 0, 0].astype(F32) + pb_in[u, 1, 0].astype(F32)
        ).astype(BF)
        for j in range(1, 4):
            send(xb.at[u, own_flat(xs[j])], xb_in.at[u, j - 1], dev(dx=j), xyr + 3 * u + j - 1)

    squares_x()
    push(PUSH[2])
    loads[1].wait()
    loads[2].wait()
    def weights_there(*numbers):
        for k in numbers:
            u, first, count = cuts[k]
            arrived(weight[u].at[1 - yh, :, pl.ds(first, count)], w_id + k)

    for u in range(2):
        weights_there(*((0, 1), (2,))[u])
        multiply_b(u)
    for g in range(2):
        weights_there(3 + g)
        multiply_a(g)
    z_step(0, 4)
    z_step(1, 4)
    weights_there(5)
    multiply_a(2)
    x_step(0)
    x_step(1)
    z_step(0, 3)
    z_step(1, 3)
    weights_there(6)
    multiply_a(3)
    send(wd_hbm.at[others], wd.at[yh], dev(dy=1), w_id + 7)
    squares_z()
    x_step(2)
    x_done(0)
    x_done(1)
    z_step(0, 2)
    x_step(3)
    z_step(1, 2)
    x_done(2)
    squares_done()
    x_done(3)
    xb_start(0)
    xb_start(1)

    def scaling(index, offset, count):
        lane_scale = squares_all[pl.ds(index, 1)]
        pick = (
            lax.broadcasted_iota(jnp.int32, (count, 128), 0) + offset
            == lax.broadcasted_iota(jnp.int32, (count, 128), 1)
        )
        return jnp.sum(jnp.where(pick, lane_scale, 0.0), axis=1, keepdims=True)

    def activate(gate, upper, scale):
        gate = gate * scale
        return (gate / (1.0 + jnp.exp(-gate)) * (upper * scale)).astype(BF)

    ga, gax = ids(8), ids(24)
    gb, gbz = ids(4), ids(8)

    scale_rows[...] = jnp.broadcast_to(scaling(z // 2, 48 * lax.rem(z, 2), 48), (48, 128)).reshape(3, 16, 128)
    sums = []
    for u in range(2):
        value = xb[u, own_flat(x)].astype(F32)
        for j in range(3):
            arrived(xb_in.at[u, j], xyr + 3 * u + j)
            value = value + xb_in[u, j].astype(F32)
        sums.append(value)
    tiles = [scale_rows[lax.rem(4 * x + i, 3)] for i in range(4)]
    act_b[z, own_flat(x)] = activate(sums[0], sums[1], jnp.concatenate(tiles, axis=0))
    for j in range(1, 4):
        send(act_b.at[z, own_flat(x)], act_b.at[z, own_flat(x)], dev(dx=j), gb + j)

    sums = []
    for u in range(2):
        value = za[u, :, z].astype(F32)
        for d in range(1, 8):
            arrived(za_in.at[u, d], zra + 8 * u + d)
            value = value + za_in[u, d].astype(F32)
        sums.append(value.reshape(96, 128))
    act_a[x, z] = activate(sums[0], sums[1], scaling(x, 0, 96))
    for d in range(1, 8):
        send(act_a.at[x, z], act_a.at[x, z], dev(dz=d), ga + d)
    for j in range(1, 4):
        send(act_a.at[x, z], act_a.at[x, z], dev(dx=j), gax + j - 1)

    for j in range(1, 4):
        arrived(act_b.at[z, own_flat(back[j])], gb + j)

    def gz_id(dist, towards):
        return gbz + 2 * (dist - 1) + (0 if towards > 0 else 1)

    for t in (1, -1):
        for dist in (2, 1):
            send(act_b.at[z], act_b.at[z], dev(dz=t * dist), gz_id(dist, t))

    def a_step(d):
        nz = zs[(8 - d) % 8]
        arrived(act_a.at[x, nz], ga + d)
        for j in range(1, 4):
            send(act_a.at[x, nz], act_a.at[x, nz], dev(dx=j), gax + 3 * d + j - 1)

    a_step(1)
    a_step(7)
    for t in (1, -1):
        far = act_b.at[zs[(8 - 2 * t) % 8]]
        arrived(far, gz_id(2, t))
        send(far, far, dev(dz=t), gz_id(3, t))
        send(far.at[half(t)], far.at[half(t)], dev(dz=2 * t), gz_id(4, t))
    for d in (2, 6, 3, 5, 4):
        a_step(d)
    for t in (1, -1):
        arrived(act_b.at[zs[(8 - t) % 8]], gz_id(1, t))
        arrived(act_b.at[zs[(8 - 3 * t) % 8]], gz_id(3, t))
        arrived(act_b.at[zs[4], half(t)], gz_id(4, t))

    loads[3].wait()
    arrived(wd.at[1 - yh], w_id + 7)

    def lower(chunks, first):
        for i in range(0, len(chunks), 2):
            pieces, numbers = zip(*chunks[i : i + 2])
            piece = jnp.concatenate(pieces, axis=1) if len(pieces) == 2 else pieces[0]
            depth = pl.ds(128 * numbers[0], 128 * len(numbers))
            for ny in range(2):
                value = jnp.dot(piece, wd[ny, depth], preferred_element_type=F32).reshape(4, 96, 256)
                if first and i == 0:
                    down[ny] = value
                else:
                    down[ny] += value

    lower([(act_b[:, 48 * c : 48 * c + 48].reshape(384, 128), NA + c) for c in range(NB)], True)
    for d in range(8):
        for j in range(1, 4):
            arrived(act_a.at[back[j], zs[(8 - d) % 8]], gax + 3 * d + j - 1)
    lower([(act_a[:, c].reshape(384, 128), c) for c in range(NA)], False)
    down_bf[...] = down[...].astype(BF)

    q3 = ids(7)
    for k, (dy, dh, ds) in enumerate(group8):
        send(down_bf.at[ys[dy], quarter(dh, ds)], down_in.at[k], dev(dy=dy, dh=dh, ds=ds), q3 + k)
    total = hidden[...] + down[yh, mine]
    for k in range(7):
        arrived(down_in.at[k], q3 + k)
        total = total + down_in[k].astype(F32)
    fin[0] = total[:, :128]
    fin[1] = total[:, 128:]

    for r in range(3):
        for j in range(2):
            value = fin[j, pl.ds(r, 32, stride=3), :]
            for k in range(4):
                send1[pl.ds((2 * r + j) * 4 + k, 8, stride=32), :] = value[8 * k : 8 * k + 8]
    for k in range(8):
        send1[pl.ds(24 + k, 8, stride=32), :] = jnp.zeros((8, 128), F32)
    send1_bf[...] = send1[...].astype(BF).reshape(8, 32, 128)
    f1 = ids(7)
    for d in range(1, 8):
        send(send1_bf.at[zs[d]], mid.at[z], dev(dz=d), f1 + d - 1)
    mid[z] = send1_bf[z]
    for d in range(1, 8):
        arrived(mid.at[zs[8 - d]], f1 + d - 1)
    mid_wide[...] = mid[...].astype(F32).reshape(256, 128)
    for k in range(4):
        rows_k = [mid_wide[pl.ds(4 * i + k, 8, stride=32), :] for i in range(6)]
        send2[k] = jnp.concatenate(rows_k, axis=0).astype(BF)

    f2 = ids(16)
    for xl in range(2):
        for ny in range(2):
            for nh in range(2):
                nx = 2 * h + xl
                own = (nx == x) & (ny == yh) & (nh == h)

                @pl.when(own)
                def _():
                    final[xy] = send2[2 * xl + ny]

                send(
                    send2.at[2 * xl + ny], final.at[xy], ((nx * 2 + ny) * 8 + z, nh, s),
                    f2 + 4 * xl + 2 * ny + nh, jnp.logical_not(own), slot=f2 + xy,
                )
    for k in range(8):
        own = (xy == k) & (h == x // 2)

        @pl.when(jnp.logical_not(own))
        def _():
            arrived(final.at[k], f2 + k)

    final_wide[...] = final[...].astype(F32).reshape(384, 128)
    for k in range(8):
        columns = [final_wide[pl.ds(48 * k + 8 * j + i, 3, stride=16), :] for i in range(8) for j in range(2)]
        out[:, 2048 * k : 2048 * k + 2048] = jnp.concatenate(columns, axis=1).astype(BF)

    for ref, index, condition in pending:
        when(condition, lambda: copy_of(ref, ref, dev(dh=1), index, index).wait_send())
    assert counter[0] <= SEMS


SEMS = 320


def layer(
    lengths, queries, new_keys, new_values, key_cache, value_cache,
    residual, gain, out_weight, gate_weight, up_weight, down_weight,
):
    vmem = pl.BlockSpec(memory_space=pltpu.VMEM)
    anywhere = pl.BlockSpec(memory_space=pl.ANY)
    scratch = [
        pltpu.VMEM((3, 2048, 256), BF),
        pltpu.VMEM((3, 2048, 256), BF),
        pltpu.VMEM((3, 2, 16, HS), BF),
        pltpu.VMEM((2048, 256), BF),
        pltpu.VMEM((2, 256, UNITS), BF),
        pltpu.VMEM((2, 256, UNITS), BF),
        pltpu.VMEM((2, UNITS, 256), BF),
        pltpu.VMEM((2, 64, 3, 16, HS), BF),
        pltpu.VMEM((64 * 3 * 16, HS), F32),
        pltpu.VMEM((4, 96, 256), F32),
        pltpu.VMEM((4, 96, 256), BF),
        pltpu.VMEM((3, 96, 256), BF),
        pltpu.VMEM((96, 256), F32),
        pltpu.VMEM((2, 4, 96, 256), BF),
        pltpu.VMEM((2, 4, 8, 128), F32),
        pltpu.VMEM((2, 8, 128), F32),
        pltpu.VMEM((10, 8, 128), F32),
        pltpu.VMEM((8, 128), F32),
        pltpu.VMEM((2, 4, 2, NA, 48, 128), BF),
        pltpu.VMEM((2, 2, NA, 48, 128), BF),
        pltpu.VMEM((2, 2, 2, NA, 48, 128), BF),
        pltpu.VMEM((2, 2, NA, 48, 128), BF),
        pltpu.VMEM((2, 8, 2, 48, 128), BF),
        pltpu.VMEM((2, 8, FLAT, 128), BF),
        pltpu.VMEM((2, 2, 4, FLAT, 128), BF),
        pltpu.VMEM((2, FLAT, 128), BF),
        pltpu.VMEM((2, 3, FLAT // 4, 128), BF),
        pltpu.VMEM((3, 16, 128), F32),
        pltpu.VMEM((4, NA, 96, 128), BF),
        pltpu.VMEM((8, FLAT, 128), BF),
        pltpu.VMEM((2, 4, 96, 256), F32),
        pltpu.VMEM((2, 4, 96, 256), BF),
        pltpu.VMEM((7, 96, 256), BF),
        pltpu.VMEM((2, 96, 128), F32),
        pltpu.VMEM((256, 128), F32),
        pltpu.VMEM((8, 32, 128), BF),
        pltpu.VMEM((8, 32, 128), BF),
        pltpu.VMEM((256, 128), F32),
        pltpu.VMEM((4, 48, 128), BF),
        pltpu.VMEM((8, 48, 128), BF),
        pltpu.VMEM((384, 128), F32),
        pltpu.SemaphoreType.DMA((6,)),
        pltpu.SemaphoreType.DMA((4,)),
        pltpu.SemaphoreType.DMA((SEMS,)),
        pltpu.SemaphoreType.DMA((SEMS,)),
    ]
    return pl.pallas_call(
        layer_kernel,
        out_shape=jax.ShapeDtypeStruct((3, D), BF),
        in_specs=[pl.BlockSpec(memory_space=pltpu.SMEM), vmem, vmem, vmem, anywhere, anywhere, vmem, vmem] + [anywhere] * 4,
        out_specs=vmem,
        scratch_shapes=scratch,
        compiler_params=pltpu.CompilerParams(collective_id=0, has_side_effects=True, vmem_limit_bytes=VMEM_LIMIT),
        cost_estimate=pl.CostEstimate(flops=2 * 384 * 256 * 12032, bytes_accessed=8 * 2**20, transcendentals=0),
        name="layer",
    )(lengths, queries, new_keys, new_values, key_cache, value_cache, residual.reshape(4, 96, 256), gain, out_weight, gate_weight, up_weight, down_weight)


def body(
    queries,
    new_keys,
    new_values,
    key_cache,
    value_cache,
    cache_lengths,
    residual,
    norm_gain,
    out_weight,
    gate_weight,
    up_weight,
    down_weight,
):
    rows = layer(
        cache_lengths, queries[0], new_keys[0], new_values[0], key_cache[0], value_cache[0],
        residual, norm_gain, out_weight, gate_weight, up_weight, down_weight,
    )
    return rows.reshape(1, 3, D)


def solution(mesh):
    return jax.shard_map(
        body,
        mesh=mesh,
        in_specs=(
            P("side", "dp", "head"),
            P("side", "dp", "head"),
            P("side", "dp", "head"),
            P("side", "dp", None, "head"),
            P("side", "dp", None, "head"),
            P("side", "dp"),
            P(None, None, "dp"),
            P("dp"),
            P(("head", "side"), "dp"),
            P("dp", ("head", "side")),
            P("dp", ("head", "side")),
            P(("head", "side"), "dp"),
        ),
        out_specs=P("side", "dp", None),
        check_vma=False,
    )
```
